256 devices in a mesh: tm: 16 (over y_lo, x, core), space: 16 (over y_hi, z).
Axes of the slice: x: 4, y: 4 (y_hi: 2, y_lo: 2; y = y_hi * 2 + y_lo), z: 8, core: 2. Of those that a mesh axis runs over, the one named last changes fastest.
Arguments:
- eigvecs: bfloat16 [16, 2, 3, 128, 36864], P('tm', None, None, None, 'space'), may hold values from -0.625 to 0.625
- links: bfloat16 [16, 3, 2, 3, 3, 36864], P('tm', None, None, None, None, 'space'), may hold values from -6 to 6
- perambulators: bfloat16 [16, 2, 2, 512, 512], P('tm'), may hold values from -0.03125 to 0.03125
- directions: int32 [4], replicated, may hold values from 0 to 3, each once
- mom_pick: int32 [4], replicated, may hold values from 0 to 6
- mom_table: int32 [7, 3], replicated, may hold values from -2 to 2
Outputs:
- elementals: float32 [4, 2, 16, 128, 128], P(None, None, 'tm', 'space')
- correlators: float32 [2, 16, 2, 4, 4], P(None, 'tm')
The draws below stay inside these ranges and needn't reach their ends.
Inputs may be any that keep to these rules, and one draw needn't show every extreme that they name: `directions`: each of the four displacement paths is used by exactly one operator.
All inputs are finite; a program needn't handle non-finite values.
Results may differ from the reference program's by a relative error of at most 0.0064.
Values may be sent and summed in bfloat16 or wider, within the bound.
A program may use at most 128 MiB of HBM per device.

```python
import math
import jax
import jax.numpy as jnp
from jax import lax

NV = 128
LXY = 48
NOPS = 4
NMOM = 7
NDT = 1
T_SIZE = 16
NZ = 16
SITES = 36864


def place_ends(values, stream_key, low, largest):
    extent = values.shape
    place = [jax.random.randint(jax.random.fold_in(stream_key, axis), (), 0, extent[axis]) for axis in range(len(extent))]
    values = values.at[tuple(place)].set(low)
    longest = extent.index(max(extent))
    place[longest] = (place[longest] + 1) % extent[longest]
    return values.at[tuple(place)].set(largest)


def levels(own_key, extent, shards, low, largest):
    def one(axis_at, parts):
        draws = jax.random.uniform(jax.random.fold_in(jax.random.fold_in(own_key, 6), axis_at), (parts,), jnp.float32, low / len(shards), largest / len(shards))
        return jnp.repeat(jnp.exp(draws), extent[axis_at] // parts).reshape((-1,) + (1,) * (len(extent) - axis_at - 1))

    loudness = one(*shards[0])
    for cut in shards[1:]:
        loudness = loudness * one(*cut)
    return loudness


def noise(rng, extent, scale, limit, pieces=(), kind=jnp.bfloat16):
    gain = levels(rng, extent, pieces, -0.22, 0.18) if pieces else 1.0
    array = jax.random.normal(rng, extent, jnp.float32) * scale * gain
    return jnp.minimum(jnp.maximum(array, -limit), limit).astype(kind)


def setup_inputs(seed: int = 0) -> dict:
    key_list = jax.random.split(jax.random.key(seed), 7)
    return {
        "eigvecs": noise(key_list[0], (T_SIZE, 2, 3, NV, SITES), ((6 * SITES) ** -0.25), 0.625, ((0, 16), (4, 16))),
        "links": noise(key_list[1], (T_SIZE, 3, 2, 3, 3, SITES), (3 ** -0.5), 6.0, ((0, 16), (5, 16))),
        "perambulators": noise(key_list[2], (T_SIZE, 2 * NDT, 2, 4 * NV, 4 * NV), (0.84 * (8 * NV * NV) ** -0.5), 0.03125, ((0, 16),)),
        "directions": jax.random.permutation(key_list[3], 4).astype(jnp.int32),
        "mom_pick": place_ends(jax.random.randint(key_list[4], (NOPS,), 0, NMOM), jax.random.fold_in(key_list[4], 1), 0, NMOM - 1).astype(jnp.int32),
        "mom_table": place_ends(jax.random.randint(key_list[5], (NMOM, 3), -2, 3), jax.random.fold_in(key_list[5], 1), -2, 2).astype(jnp.int32),
    }


def apply_link(link_re, link_im, vec_re, vec_im):
    out_re = 0.0
    out_im = 0.0
    for column in range(3):
        left_re = link_re[:, column][:, None, :]
        left_im = link_im[:, column][:, None, :]
        out_re = out_re + left_re * vec_re[column][None] - left_im * vec_im[column][None]
        out_im = out_im + left_re * vec_im[column][None] + left_im * vec_re[column][None]
    return out_re, out_im


def apply_dagger(link_re, link_im, vec_re, vec_im):
    out_re = 0.0
    out_im = 0.0
    for column in range(3):
        left_re = link_re[column][:, None, :]
        left_im = link_im[column][:, None, :]
        out_re = out_re + left_re * vec_re[column][None] + left_im * vec_im[column][None]
        out_im = out_im + left_re * vec_im[column][None] - left_im * vec_re[column][None]
    return out_re, out_im


def to_grid(values):
    return values.reshape(values.shape[:-1] + (NZ, LXY, LXY))


def to_flat(values):
    return values.reshape(values.shape[:-3] + (SITES,))


def slice_elementals(vectors, gauge_field, directions, cosine, sine_part):
    vec_f = vectors.astype(jnp.float32)
    candidates = [vec_f]
    for direction in range(3):
        axis_pos = -1 - direction
        link_re = gauge_field[direction, 0].astype(jnp.float32)
        link_im = gauge_field[direction, 1].astype(jnp.float32)
        back_re, back_im = apply_dagger(link_re, link_im, vec_f[0], vec_f[1])
        back_all = lax.optimization_barrier(jnp.stack([back_re, back_im]).astype(jnp.bfloat16))
        ahead = to_flat(jnp.roll(to_grid(vectors), -1, axis_pos)).astype(jnp.float32)
        behind = to_flat(jnp.roll(to_grid(back_all), 1, axis_pos)).astype(jnp.float32)
        fwd_re, fwd_im = apply_link(link_re, link_im, ahead[0], ahead[1])
        candidates.append(jnp.stack([fwd_re - behind[0], fwd_im - behind[1]]))
    chosen = jnp.take(jnp.stack(candidates), directions, axis=0)
    phased_re = (cosine * chosen[:, 0] + sine_part * chosen[:, 1]).astype(jnp.bfloat16).astype(jnp.float32)
    phased_im = (cosine * chosen[:, 1] - sine_part * chosen[:, 0]).astype(jnp.bfloat16).astype(jnp.float32)
    form = 'ckn,ocln->okl'
    elem_re = jnp.einsum(form, vec_f[0], phased_re) + jnp.einsum(form, vec_f[1], phased_im)
    elem_im = jnp.einsum(form, vec_f[0], phased_im) - jnp.einsum(form, vec_f[1], phased_re)
    return jnp.stack([elem_re, elem_im], axis=1)


def contract_all(tile, sink_elem, source_elem, gamma_sign):
    vector_count = sink_elem.shape[-1]
    spin_width = 4 * vector_count
    tile_f = tile.astype(jnp.float32)
    sink_f = sink_elem.astype(jnp.float32)
    source_f = source_elem.astype(jnp.float32)
    count = sink_f.shape[0]

    def left_product(elem, block):
        return jnp.einsum('okl,blc->obkc', elem, block.reshape(4, vector_count, spin_width)).reshape(count, spin_width, spin_width)

    def right_product(block, elem):
        return jnp.einsum('ral,qkl->qrak', block.reshape(spin_width, 4, vector_count), elem).reshape(count, spin_width, spin_width)

    x_re = left_product(sink_f[:, 0], tile_f[0]) - left_product(sink_f[:, 1], tile_f[1])
    x_im = left_product(sink_f[:, 0], tile_f[1]) + left_product(sink_f[:, 1], tile_f[0])
    z_re = (right_product(tile_f[0], source_f[:, 0]) + right_product(tile_f[1], source_f[:, 1])) * gamma_sign[None, :, None]
    z_im = (right_product(tile_f[0], source_f[:, 1]) - right_product(tile_f[1], source_f[:, 0])) * gamma_sign[None, :, None]
    high = lax.Precision.HIGHEST
    form = 'orc,qrc->oq'
    corr_re = jnp.einsum(form, x_re, z_re, precision=high) - jnp.einsum(form, x_im, z_im, precision=high)
    corr_im = jnp.einsum(form, x_re, z_im, precision=high) + jnp.einsum(form, x_im, z_re, precision=high)
    return jnp.stack([corr_re, corr_im])


def reference(eigvecs, links, perambulators, directions, mom_pick, mom_table):
    site_index = jnp.arange(SITES, dtype=jnp.int32)
    coord_x = (site_index % LXY).astype(jnp.float32)
    coord_y = ((site_index // LXY) % LXY).astype(jnp.float32)
    coord_z = (site_index // (LXY * LXY)).astype(jnp.float32)
    momenta = jnp.take(mom_table, mom_pick, axis=0).astype(jnp.float32)
    phase_angle = 2.0 * math.pi * (momenta[:, 0:1] * coord_x[None] / LXY + momenta[:, 1:2] * coord_y[None] / LXY + momenta[:, 2:3] * coord_z[None] / NZ)
    cosine = jnp.cos(phase_angle)[:, None, None, :]
    sine_part = jnp.sin(phase_angle)[:, None, None, :]

    def one_slice(pair):
        return slice_elementals(pair[0], pair[1], directions, cosine, sine_part)

    slices = lax.map(one_slice, (eigvecs, links))
    elementals = jnp.transpose(slices, (1, 2, 0, 3, 4))
    rounded = slices.astype(jnp.bfloat16)
    gamma_sign = jnp.where(jnp.arange(4 * NV, dtype=jnp.int32) // NV < 2, 1.0, -1.0).astype(jnp.float32)

    def one_sink(sink):
        results = []
        for offset in range(2 * NDT):
            distance = offset + 1 if offset < NDT else -(offset - NDT + 1)
            source = (sink - distance) % T_SIZE
            results.append(contract_all(perambulators[sink, offset], rounded[sink], rounded[source], gamma_sign))
        return jnp.stack(results, axis=1)

    corr = lax.map(one_sink, jnp.arange(T_SIZE, dtype=jnp.int32))
    return elementals, jnp.transpose(corr, (1, 0, 2, 3, 4))
```

```python
import functools
import math

import jax
import jax.numpy as jnp
from jax import lax
from jax.experimental import pallas as pl
from jax.experimental.pallas import tpu as pltpu
from jax.sharding import PartitionSpec as P

LXY = 48
MESH = pl.DeviceIdType.MESH
F32 = jnp.float32
BF16 = jnp.bfloat16
NT = (((1,), (1,)), ((), ()))
LANES = 128
HALF = 9
BLOCKS = 18
NV = 128
ROWS = 8


def dot_nt(a, b):
    return lax.dot_general(a, b, NT, preferred_element_type=F32)


def kernel(n_tm, n_space, eig, links, tau, dirs, pick, table, elem_out, corr_out,
           vbuf, rdn, rup, lk, lkup, lkf, lkupf, ph, lhs, rhs, acc0, accd, part,
           rs_send, rs_recv, own, ag_send, ag, tauo, taun, zbuf, wmat, rowbuf,
           ps_send, ps_own, ps_even, local_sem, halo_send, halo_recv, lk_sem, tau_sem,
           rs_sem, ag_sem, ps_sem, go_sem):
    t = lax.axis_index("tm")
    me = lax.axis_index("space")
    odd = lax.rem(t, 2) == 1
    even = lax.rem(t, 2) == 0
    t_next = lax.rem(t + 1, n_tm)
    t_prev = lax.rem(t + n_tm - 1, n_tm)
    up = lax.rem(me + 1, n_space)
    down = lax.rem(me + n_space - 1, n_space)

    def dev(a, b):
        return {"tm": a, "space": b}

    def remote(src, dst, ssem, rsem, where):
        return pltpu.make_async_remote_copy(
            src_ref=src, dst_ref=dst, send_sem=ssem, recv_sem=rsem,
            device_id=where, device_id_type=MESH)

    def wait_bytes(ref, sem):
        pltpu.make_async_copy(ref, ref, sem).wait()

    def load_block(j):
        return pltpu.make_async_copy(
            eig.at[0, :, :, :, pl.ds(pl.multiple_of(j * LANES, LANES), LANES)],
            vbuf.at[j], local_sem.at[0])

    pltpu.make_async_copy(links.at[0], lk, local_sem.at[1]).start()

    def start_load(j, carry):
        load_block(j).start()
        return carry

    lax.fori_loop(0, BLOCKS, start_load, 0)
    pltpu.make_async_copy(tau.at[0], tauo, local_sem.at[2]).start()

    barrier = pltpu.get_barrier_semaphore()

    def greet(a, b):
        pl.semaphore_signal(barrier, inc=1, device_id=dev(a, b), device_id_type=MESH)

    greet(t, up)
    greet(t, down)

    def greet_group(k, carry):
        greet(t, lax.rem(me + k, n_space))
        return carry

    lax.fori_loop(2, n_space - 1, greet_group, 0)

    def greet_near(k, carry):
        greet(t_next, k)
        greet(t_prev, k)
        return carry

    lax.fori_loop(0, n_space, greet_near, 0)
    pl.semaphore_wait(barrier, 3 * n_space - 1)

    def halo(n, side):
        j = n + HALF * side
        return remote(
            eig.at[0, :, :, :, pl.ds(pl.multiple_of(j * LANES, LANES), LANES)],
            (rup if side else rdn).at[n], halo_send.at[side, n], halo_recv.at[side, n],
            dev(t, up if side else down))

    def start_halo(n, carry):
        halo(n, 0).start()
        halo(n, 1).start()
        return carry

    link_copy = remote(links.at[0, 2, :, :, :, pl.ds(HALF * LANES, HALF * LANES)], lkup,
                       lk_sem.at[0], lk_sem.at[1], dev(t, up))
    link_copy.start()

    @pl.when(even)
    def _():
        lax.fori_loop(0, HALF, start_halo, 0)
        remote(tau.at[0, 0], taun.at[0], tau_sem.at[0], tau_sem.at[2], dev(t_prev, me)).start()
        remote(tau.at[0, 1], taun.at[1], tau_sem.at[1], tau_sem.at[3], dev(t_next, me)).start()

    site = (lax.broadcasted_iota(jnp.int32, (24, LANES), 0) * LANES
            + lax.broadcasted_iota(jnp.int32, (24, LANES), 1)).astype(F32)
    site_y = jnp.floor((site + 0.5) * (1.0 / LXY))
    site_x = site - site_y * LXY

    def spread_scalar(value):
        return jnp.full((1, LANES), value, jnp.int32)

    picked = []
    for o in range(4):
        choice = spread_scalar(pick[o])
        row = [jnp.zeros((1, LANES), jnp.int32)] * 3
        for r in range(table.shape[0]):
            row = [jnp.where(choice == r, spread_scalar(table[r, axis]), row[axis]) for axis in range(3)]
        picked.append(row)

    def path_momentum(path, axis):
        total = jnp.zeros((1, LANES), jnp.int32)
        for o in range(4):
            total = jnp.where(spread_scalar(dirs[o]) == path, picked[o][axis], total)
        return total.astype(F32)

    mom = [[path_momentum(path, axis) for axis in range(3)] for path in range(4)]
    extent_z = 1.0 * n_space
    plane = me.astype(F32)
    for path in range(4):
        flat = 2.0 * math.pi * (mom[path][0] * site_x / LXY + mom[path][1] * site_y / LXY
                                + mom[path][2] * plane / extent_z)
        ph[path, 0] = jnp.cos(flat)
        ph[path, 1] = jnp.sin(flat)
    flat = 2.0 * math.pi * (mom[3][0] * site_x / LXY + mom[3][1] * site_y / LXY
                            + mom[3][2] * (plane - 1.0) / extent_z)
    ph[4, 0] = jnp.cos(flat)
    ph[4, 1] = jnp.sin(flat)

    wait_bytes(lk, local_sem.at[1])
    for d in range(3):
        for ri in range(2):
            for c in range(3):
                lkf[d, ri, c] = lk[d, ri, c].astype(F32)
    wait_bytes(vbuf, local_sem.at[0])

    acc0[...] = jnp.zeros_like(acc0)
    accd[...] = jnp.zeros_like(accd)
    lane = lax.broadcasted_iota(jnp.int32, (NV, LANES), 1)

    def link_rows(ref_row):
        return [[[jnp.broadcast_to(ref_row(ri, c, a), (16, LANES)) for a in range(3)]
                 for c in range(3)] for ri in range(2)]

    def back_block(vref, u, cosine, sine, slot):
        cosine = jnp.broadcast_to(cosine, (16, LANES))
        sine = jnp.broadcast_to(sine, (16, LANES))

        def tile(k, carry):
            at = pl.multiple_of(k * 16, 16)
            v = [[vref[ri, c, pl.ds(at, 16), :].astype(F32) for c in range(3)] for ri in range(2)]
            for a in range(3):
                b_re = u[0][0][a] * v[0][0] + u[1][0][a] * v[1][0]
                b_im = u[0][0][a] * v[1][0] - u[1][0][a] * v[0][0]
                for c in (1, 2):
                    b_re = b_re + u[0][c][a] * v[0][c] + u[1][c][a] * v[1][c]
                    b_im = b_im + u[0][c][a] * v[1][c] - u[1][c][a] * v[0][c]
                col = pl.ds((slot * 3 + a) * LANES, LANES)
                lhs[pl.ds(at, 16), col] = (cosine * b_re).astype(BF16)
                lhs[pl.ds(at + 128, 16), col] = (cosine * b_im).astype(BF16)
                lhs[pl.ds(at + 256, 16), col] = (sine * b_re).astype(BF16)
                lhs[pl.ds(at + 384, 16), col] = (sine * b_im).astype(BF16)
            return carry

        lax.fori_loop(0, NV // 16, tile, 0, unroll=2)

    def own_links(d, j):
        at = pl.ds(pl.multiple_of(j * LANES, LANES), LANES)
        return link_rows(lambda ri, c, a: lkf[d, ri, c, a:a + 1, at])

    def plain_block(j, slot):
        cosine = jnp.broadcast_to(ph[0, 0, pl.ds(j, 1), :], (16, LANES))
        sine = jnp.broadcast_to(ph[0, 1, pl.ds(j, 1), :], (16, LANES))

        def tile(k, carry):
            at = pl.multiple_of(k * 16, 16)
            for c in range(3):
                v_re = vbuf[j, 0, c, pl.ds(at, 16), :].astype(F32)
                v_im = vbuf[j, 1, c, pl.ds(at, 16), :].astype(F32)
                col = pl.ds((slot * 3 + c) * LANES, LANES)
                rhs[pl.ds(at, 16), col] = (cosine * v_re + sine * v_im).astype(BF16)
                rhs[pl.ds(at + 128, 16), col] = (cosine * v_im - sine * v_re).astype(BF16)
            return carry

        lax.fori_loop(0, NV // 16, tile, 0, unroll=2)

    def ahead_block(d, j, slot):
        after = jnp.where(j == BLOCKS - 1, 0, j + 1)
        before = jnp.where(j == 0, BLOCKS - 1, j - 1)
        if d == 0:
            edge = lax.rem(j * LANES + lane, LXY) == LXY - 1
        for ri in range(2):
            for c in range(3):
                here = vbuf[j, ri, c]
                there = vbuf[after, ri, c]
                if d == 1:
                    turned = jnp.where(lane < LANES - LXY, pltpu.roll(here, LANES - LXY, 1),
                                       pltpu.roll(there, LANES - LXY, 1))
                else:
                    back = vbuf[before, ri, c]
                    near = jnp.where(lane == LANES - 1, pltpu.roll(there, LANES - 1, 1),
                                     pltpu.roll(here, LANES - 1, 1))
                    far = jnp.where(lane < LXY - 1, pltpu.roll(back, LXY - 1, 1),
                                    pltpu.roll(here, LXY - 1, 1))
                    turned = jnp.where(edge, far, near)
                rhs[pl.ds(ri * 128, 128), pl.ds((slot * 3 + c) * LANES, LANES)] = turned

    def stacked(parts):
        return jnp.concatenate(
            [jnp.concatenate([p[ri, c] for p in parts for c in range(3)], axis=1) for ri in range(2)],
            axis=0)

    def local_pair(i, carry):
        j = 2 * i
        for s in range(2):
            plain_block(j + s, s)
        acc0[...] += dot_nt(stacked([vbuf.at[j], vbuf.at[j + 1]]), rhs[...])
        for d in range(2):
            for s in range(2):
                back_block(vbuf.at[j + s], own_links(d, j + s), ph[d + 1, 0, pl.ds(j + s, 1), :],
                           ph[d + 1, 1, pl.ds(j + s, 1), :], s)
                ahead_block(d, j + s, s)
            accd[d] += dot_nt(lhs[...], rhs[...])
        return carry

    lax.fori_loop(0, BLOCKS // 2, local_pair, 0)

    def blocks_of(ref, row):
        g_rr = ref[row:row + 128, 0:128]
        g_ri = ref[row:row + 128, 128:256]
        g_ir = ref[row + 128:row + 256, 0:128]
        g_ii = ref[row + 128:row + 256, 128:256]
        return g_rr + g_ii, g_ri - g_ir

    def finish_direction(d):
        c_re, c_im = blocks_of(accd.at[d], 0)
        s_re, s_im = blocks_of(accd.at[d], 256)
        length = (float(LXY), float(LXY), extent_z)[d]
        turn = jnp.full((1, LANES), 2.0 * math.pi / length, F32) * mom[d + 1][d]
        cosine = jnp.cos(turn)
        sine = jnp.sin(turn)
        p_re = c_re - s_im
        p_im = c_im + s_re
        n_re = cosine * p_re - sine * p_im
        n_im = sine * p_re + cosine * p_im
        part[d + 1, 0] = c_re + s_im - n_re.T
        part[d + 1, 1] = c_im - s_re + n_im.T

    part[0, 0], part[0, 1] = blocks_of(acc0, 0)
    finish_direction(0)
    finish_direction(1)

    def spread(first, count, which):
        width = 16 * count
        for j in range(n_space):
            for p in range(count):
                for ri in range(2):
                    own[which, pl.ds(p * 16 + ri * 8, 8), :] = part[first + p, ri, j * 8:(j + 1) * 8, :]
            rs_send[which, j, 0:width, :] = own[which, 0:width, :].astype(BF16)
        for p in range(count):
            for ri in range(2):
                own[which, pl.ds(p * 16 + ri * 8, 8), :] = part[
                    first + p, ri, pl.ds(pl.multiple_of(me * 8, 8), 8), :]

        def send(k, carry):
            j = lax.rem(me + k, n_space)
            remote(rs_send.at[which, j, pl.ds(0, width)], rs_recv.at[which, k - 1, pl.ds(0, width)],
                   rs_sem.at[which, 0], rs_sem.at[which, 1], dev(t, j)).start()
            return carry

        lax.fori_loop(1, n_space, send, 0)

    def gather(which, width):
        wait_bytes(rs_recv.at[which, :, pl.ds(0, width)], rs_sem.at[which, 1])
        total = own[which, 0:width, :]
        for k in range(n_space - 1):
            total = total + rs_recv[which, k, 0:width, :].astype(F32)
        own[which, 0:width, :] = total

    def publish(which, width):
        ag_send[which, 0:width, :] = own[which, 0:width, :].astype(BF16)

        def send(j, carry):
            remote(ag_send.at[which, pl.ds(0, width)], ag.at[which, 0, me, pl.ds(0, width)],
                   ag_sem.at[which, 0], ag_sem.at[which, 1], dev(t_next, j)).start()
            remote(ag_send.at[which, pl.ds(0, width)], ag.at[which, 1, me, pl.ds(0, width)],
                   ag_sem.at[which, 0], ag_sem.at[which, 1], dev(t_prev, j)).start()
            return carry

        lax.fori_loop(0, n_space, send, 0)

    spread(0, 3, 0)

    link_copy.wait()
    for ri in range(2):
        for c in range(3):
            lkupf[ri, c] = lkup[ri, c].astype(F32)

    def z_block(n, carry):
        halo(n, 0).wait_recv()
        halo(n, 1).wait_recv()
        at = pl.ds(pl.multiple_of(n * LANES, LANES), LANES)
        back_block(vbuf.at[n], own_links(2, n), ph[3, 0, pl.ds(n, 1), :], ph[3, 1, pl.ds(n, 1), :], 0)
        u = link_rows(lambda ri, c, a: lkupf[ri, c, a:a + 1, at])
        m = n + HALF
        back_block(rup.at[n], u, ph[4, 0, pl.ds(m, 1), :], ph[4, 1, pl.ds(m, 1), :], 1)
        accd[2] += dot_nt(lhs[...], stacked([rdn.at[n], vbuf.at[m]]))
        return carry

    def wait_halo_sends(lo, hi):
        def one(n, carry):
            halo(n, 0).wait_send()
            halo(n, 1).wait_send()
            return carry

        lax.fori_loop(lo, hi, one, 0)

    def weights(kind, e, which, slot, path):
        src = 0 if e == 0 else 1
        if kind == 1:
            src = 1 - e
        re_rows, im_rows = [], []
        at = pl.multiple_of(slot * 16, 16)
        for j in range(n_space):
            both = ag[which, src, j, pl.ds(at, 16), :].astype(F32)
            re_rows.append(both[0:8])
            im_rows.append(both[8:16])
        phi_re = jnp.concatenate(re_rows, axis=0)
        phi_im = jnp.concatenate(im_rows, axis=0)
        if kind == 0:
            first = jnp.concatenate([phi_re, phi_im], axis=1)
            second = jnp.concatenate([phi_im, -phi_re], axis=1)
        else:
            first = jnp.concatenate([phi_re, -phi_im], axis=1)
            second = jnp.concatenate([phi_im, phi_re], axis=1)
        phi = jnp.concatenate([first, second], axis=0).astype(BF16)
        mat = tauo.at[e] if kind == 0 else taun.at[e]
        for c in range(4):
            col = slice(c * 128, (c + 1) * 128)
            z = dot_nt(jnp.concatenate([mat[0, :, col], mat[1, :, col]], axis=1), phi)
            if kind == 1 and c >= 2:
                z = -z
            zbuf[0, :, col] = z[:, 0:128].astype(BF16)
            zbuf[1, :, col] = z[:, 128:256].astype(BF16)
        total = None
        for r in range(4):
            row = slice(r * 128, (r + 1) * 128)
            g = dot_nt(jnp.concatenate([zbuf[0, row, :], zbuf[1, row, :]], axis=0),
                       jnp.concatenate([mat[0, row, :], mat[1, row, :]], axis=0))
            if total is None:
                total = g
            elif kind == 0 and r >= 2:
                total = total - g
            else:
                total = total + g
        rr, ri_, ir, ii = (total[0:128, 0:128], total[0:128, 128:256],
                           total[128:256, 0:128], total[128:256, 128:256])
        if kind == 0:
            wmat[kind, e, path, 0] = rr - ii
            wmat[kind, e, path, 1] = ri_ + ir
        else:
            wmat[kind, e, path, 0] = rr + ii
            wmat[kind, e, path, 1] = ir - ri_

    def weights_of(which, count, first):
        for kind in range(2):
            for e in range(2):
                def one(slot, carry, kind=kind, e=e):
                    weights(kind, e, which, slot, first + slot)
                    return carry

                lax.fori_loop(0, count, one, 0)

    def pair_rows(paths, lo, hi):
        for kind in range(2):
            for e in range(2):
                for p in paths:
                    def one(w, carry, kind=kind, e=e, p=p):
                        w_re, w_im = wmat[kind, e, w, 0], wmat[kind, e, w, 1]
                        p_re, p_im = part[p, 0], part[p, 1]
                        re = jnp.sum(p_re * w_re - p_im * w_im, axis=0, keepdims=True)
                        im = jnp.sum(p_re * w_im + p_im * w_re, axis=0, keepdims=True)
                        if kind == 0:
                            rowbuf[kind, w, pl.ds(e * 4 + p, 1), :] = re
                            rowbuf[kind, w, pl.ds(8 + e * 4 + p, 1), :] = im
                        else:
                            rowbuf[kind, p, pl.ds(e * 4 + w, 1), :] = re
                            rowbuf[kind, p, pl.ds(8 + e * 4 + w, 1), :] = im
                        return carry

                    lax.fori_loop(lo, hi, one, 0)

    def write_elementals():
        for o in range(4):
            path = jnp.full((8, LANES), dirs[o], jnp.int32)
            for ri in range(2):
                rows = own[1, ri * 8:(ri + 1) * 8, :]
                for p in range(3):
                    rows = jnp.where(path == p, own[0, p * 16 + ri * 8:p * 16 + ri * 8 + 8, :], rows)
                elem_out[o, ri, 0] = rows

    def write_correlators(total):
        col = lax.broadcasted_iota(jnp.int32, (16, LANES), 1)
        turned = jnp.zeros((16, LANES), F32)
        for q in range(4):
            one = jnp.sum(jnp.where(col == spread_scalar(dirs[q]), total, 0.0), axis=1, keepdims=True)
            turned = jnp.where(col == q, one, turned)
        for o in range(4):
            path = jnp.full((1, LANES), dirs[o], jnp.int32)
            for ri in range(2):
                for e in range(2):
                    at = ri * 8 + e * 4
                    row = turned[at:at + 1]
                    for p in range(1, 4):
                        row = jnp.where(path == p, turned[at + p:at + p + 1], row)
                    corr_out[ri, 0, e, o:o + 1, :] = row[:, 0:4]

    @pl.when(even)
    def _():
        lax.fori_loop(0, HALF - 2, z_block, 0)
        wait_halo_sends(0, HALF - 1)
        pl.semaphore_signal(go_sem, inc=1, device_id=dev(t_next, me), device_id_type=MESH)
        gather(0, 48)
        publish(0, 48)
        lax.fori_loop(HALF - 2, HALF, z_block, 0)
        finish_direction(2)
        spread(3, 1, 1)
        gather(1, 16)
        publish(1, 16)
        write_elementals()
        wait_halo_sends(HALF - 1, HALF)
        wait_bytes(taun.at[0], tau_sem.at[0])
        wait_bytes(taun.at[1], tau_sem.at[1])
        wait_bytes(rs_recv.at[0, :, pl.ds(0, 48)], rs_sem.at[0, 0])
        wait_bytes(rs_recv.at[1, :, pl.ds(0, 16)], rs_sem.at[1, 0])
        wait_bytes(ag.at[0, :, :, pl.ds(0, 48)], ag_sem.at[0, 0])
        wait_bytes(ag.at[1, :, :, pl.ds(0, 16)], ag_sem.at[1, 0])
        wait_bytes(ps_even, ps_sem.at[2])
        row = lax.broadcasted_iota(jnp.int32, (16, LANES), 0)
        first = ps_even[0, 0]
        second = ps_even[1, 0]
        for j in range(1, n_space):
            first = first + ps_even[0, j]
            second = second + ps_even[1, j]
        write_correlators(jnp.where(lax.rem(row, 8) < 4, first, second))

    @pl.when(odd)
    def _():
        pl.semaphore_wait(go_sem, 1)
        lax.fori_loop(0, HALF, start_halo, 0)
        gather(0, 48)
        lax.fori_loop(0, 2, z_block, 0)
        wait_bytes(taun.at[0], tau_sem.at[2])
        wait_bytes(taun.at[1], tau_sem.at[3])
        wait_bytes(tauo, local_sem.at[2])
        for e in range(2):
            for ri in range(2):
                taun[e, ri] = taun[e, ri].T
        wait_bytes(ag.at[0, :, :, pl.ds(0, 48)], ag_sem.at[0, 1])
        weights_of(0, 3, 0)
        lax.fori_loop(2, 5, z_block, 0)
        pair_rows((0, 1, 2), 0, 3)
        lax.fori_loop(5, HALF - 1, z_block, 0)
        wait_bytes(ag.at[1, :, :, pl.ds(0, 16)], ag_sem.at[1, 1])
        weights_of(1, 1, 3)
        pair_rows((0, 1, 2), 3, 4)
        lax.fori_loop(HALF - 1, HALF, z_block, 0)
        finish_direction(2)
        spread(3, 1, 1)
        pair_rows((3,), 0, 4)
        col = lax.broadcasted_iota(jnp.int32, (16, LANES), 1)
        for kind in range(2):
            tile = jnp.zeros((16, LANES), F32)
            for q in range(4):
                tile = jnp.where(col == q, jnp.sum(rowbuf[kind, q], axis=1, keepdims=True), tile)
            ps_send[kind] = tile

        def send_group(k, carry):
            remote(ps_send.at[0], ps_own.at[k - 1], ps_sem.at[0], ps_sem.at[1],
                   dev(t, lax.rem(me + k, n_space))).start()
            return carry

        def send_near(j, carry):
            remote(ps_send.at[1], ps_even.at[0, me], ps_sem.at[3], ps_sem.at[2], dev(t_next, j)).start()
            remote(ps_send.at[1], ps_even.at[1, me], ps_sem.at[3], ps_sem.at[2], dev(t_prev, j)).start()
            return carry

        lax.fori_loop(1, n_space, send_group, 0)
        lax.fori_loop(0, n_space, send_near, 0)
        gather(1, 16)
        write_elementals()
        wait_halo_sends(0, HALF)
        wait_bytes(rs_recv.at[0, :, pl.ds(0, 48)], rs_sem.at[0, 0])
        wait_bytes(rs_recv.at[1, :, pl.ds(0, 16)], rs_sem.at[1, 0])
        wait_bytes(ps_own, ps_sem.at[1])
        total = ps_send[0]
        for k in range(n_space - 1):
            total = total + ps_own[k]
        wait_bytes(ps_own, ps_sem.at[0])
        wait_bytes(ps_even, ps_sem.at[3])
        write_correlators(total)

    @pl.when(even)
    def _():
        wait_bytes(tauo, local_sem.at[2])


def solution(mesh):
    n_tm, n_space = mesh.shape["tm"], mesh.shape["space"]
    placed = (
        P("tm", None, None, None, "space"),
        P("tm", None, None, None, None, "space"),
        P("tm", None, None, None, None),
        P(),
        P(),
        P(),
    )

    def body(eigvecs, links, perambulators, directions, mom_pick, mom_table):
        hbm = pl.BlockSpec(memory_space=pl.ANY)
        smem = pl.BlockSpec(memory_space=pltpu.SMEM)
        vmem = pl.BlockSpec(memory_space=pltpu.VMEM)
        dma = pltpu.SemaphoreType.DMA
        return pl.pallas_call(
            functools.partial(kernel, n_tm, n_space),
            out_shape=(
                jax.ShapeDtypeStruct((4, 2, 1, ROWS, NV), F32),
                jax.ShapeDtypeStruct((2, 1, 2, 4, 4), F32),
            ),
            in_specs=[hbm, hbm, hbm, smem, smem, smem],
            out_specs=(vmem, vmem),
            scratch_shapes=[
                pltpu.VMEM((BLOCKS, 2, 3, NV, LANES), BF16),
                pltpu.VMEM((HALF, 2, 3, NV, LANES), BF16),
                pltpu.VMEM((HALF, 2, 3, NV, LANES), BF16),
                pltpu.VMEM((3, 2, 3, 3, BLOCKS * LANES), BF16),
                pltpu.VMEM((2, 3, 3, HALF * LANES), BF16),
                pltpu.VMEM((3, 2, 3, 3, BLOCKS * LANES), F32),
                pltpu.VMEM((2, 3, 3, HALF * LANES), F32),
                pltpu.VMEM((5, 2, 24, LANES), F32),
                pltpu.VMEM((512, 768), BF16),
                pltpu.VMEM((256, 768), BF16),
                pltpu.VMEM((256, 256), F32),
                pltpu.VMEM((3, 512, 256), F32),
                pltpu.VMEM((4, 2, NV, NV), F32),
                pltpu.VMEM((2, n_space, 48, NV), BF16),
                pltpu.VMEM((2, n_space - 1, 48, NV), BF16),
                pltpu.VMEM((2, 48, NV), F32),
                pltpu.VMEM((2, 48, NV), BF16),
                pltpu.VMEM((2, 2, n_space, 48, NV), BF16),
                pltpu.VMEM((2, 2, 512, 512), BF16),
                pltpu.VMEM((2, 2, 512, 512), BF16),
                pltpu.VMEM((2, 512, 512), BF16),
                pltpu.VMEM((2, 2, 4, 2, NV, NV), F32),
                pltpu.VMEM((2, 4, 16, NV), F32),
                pltpu.VMEM((2, 16, NV), F32),
                pltpu.VMEM((n_space - 1, 16, NV), F32),
                pltpu.VMEM((2, n_space, 16, NV), F32),
                dma((3,)),
                dma((2, HALF)),
                dma((2, HALF)),
                dma((2,)),
                dma((4,)),
                dma((2, 2)),
                dma((2, 2)),
                dma((4,)),
                pltpu.SemaphoreType.REGULAR,
            ],
            compiler_params=pltpu.CompilerParams(
                collective_id=0, has_side_effects=True, vmem_limit_bytes=48 << 20),
            name="elementals_and_correlators",
        )(eigvecs, links, perambulators, directions, mom_pick, mom_table)

    return jax.shard_map(
        body,
        mesh=mesh,
        in_specs=placed,
        out_specs=(P(None, None, "tm", "space", None), P(None, "tm", None, None, None)),
        check_vma=False,
    )
```

```python
import functools
import math

import jax
import jax.numpy as jnp
from jax import lax
from jax.experimental import pallas as pl
from jax.experimental.pallas import tpu as pltpu
from jax.sharding import PartitionSpec as P

LXY = 48
MESH = pl.DeviceIdType.MESH
F32 = jnp.float32
BF16 = jnp.bfloat16
NT = (((1,), (1,)), ((), ()))
LANES = 128
HALF = 9
BLOCKS = 18
NV = 128
ROWS = 8


def dot_nt(a, b):
    return lax.dot_general(a, b, NT, preferred_element_type=F32)


def kernel(n_tm, n_space, eig, links, tau, dirs, pick, table, elem_out, corr_out,
           vbuf, rdn, rup, lk, lkup, lkf, lkupf, ph, lhs, lhs2, lhsz, acc, accz, part,
           rs_send, rs_recv, own, ag_send, ag, tauo, taun, zbuf, wmat, rowbuf,
           ps_send, ps_own, ps_even, local_sem, halo_send, halo_recv, lk_sem, tau_sem,
           rs_sem, ag_sem, ps_sem, go_sem):
    t = lax.axis_index("tm")
    me = lax.axis_index("space")
    odd = lax.rem(t, 2) == 1
    even = lax.rem(t, 2) == 0
    t_next = lax.rem(t + 1, n_tm)
    t_prev = lax.rem(t + n_tm - 1, n_tm)
    up = lax.rem(me + 1, n_space)
    down = lax.rem(me + n_space - 1, n_space)

    def dev(a, b):
        return {"tm": a, "space": b}

    def remote(src, dst, ssem, rsem, where):
        return pltpu.make_async_remote_copy(
            src_ref=src, dst_ref=dst, send_sem=ssem, recv_sem=rsem,
            device_id=where, device_id_type=MESH)

    def wait_bytes(ref, sem):
        pltpu.make_async_copy(ref, ref, sem).wait()

    def load_block(j):
        return pltpu.make_async_copy(
            eig.at[0, :, :, :, pl.ds(pl.multiple_of(j * LANES, LANES), LANES)],
            vbuf.at[j], local_sem.at[0])

    pltpu.make_async_copy(links.at[0], lk, local_sem.at[1]).start()

    def start_load(j, carry):
        load_block(j).start()
        return carry

    lax.fori_loop(0, BLOCKS, start_load, 0)
    pltpu.make_async_copy(tau.at[0], tauo, local_sem.at[2]).start()

    barrier = pltpu.get_barrier_semaphore()

    def greet(a, b):
        pl.semaphore_signal(barrier, inc=1, device_id=dev(a, b), device_id_type=MESH)

    greet(t, up)
    greet(t, down)

    def greet_group(k, carry):
        greet(t, lax.rem(me + k, n_space))
        return carry

    lax.fori_loop(2, n_space - 1, greet_group, 0)

    def greet_near(k, carry):
        greet(t_next, k)
        greet(t_prev, k)
        return carry

    lax.fori_loop(0, n_space, greet_near, 0)
    pl.semaphore_wait(barrier, 3 * n_space - 1)

    def halo(n, side):
        j = n + HALF * side
        return remote(
            eig.at[0, :, :, :, pl.ds(pl.multiple_of(j * LANES, LANES), LANES)],
            (rup if side else rdn).at[n], halo_send.at[side, n], halo_recv.at[side, n],
            dev(t, up if side else down))

    def start_halo(n, carry):
        halo(n, 0).start()
        halo(n, 1).start()
        return carry

    link_copy = remote(links.at[0, 2, :, :, :, pl.ds(HALF * LANES, HALF * LANES)], lkup,
                       lk_sem.at[0], lk_sem.at[1], dev(t, up))
    link_copy.start()

    @pl.when(even)
    def _():
        lax.fori_loop(0, HALF, start_halo, 0)
        remote(tau.at[0, 0], taun.at[0], tau_sem.at[0], tau_sem.at[2], dev(t_prev, me)).start()
        remote(tau.at[0, 1], taun.at[1], tau_sem.at[1], tau_sem.at[3], dev(t_next, me)).start()

    site = (lax.broadcasted_iota(jnp.int32, (24, LANES), 0) * LANES
            + lax.broadcasted_iota(jnp.int32, (24, LANES), 1)).astype(F32)
    site_y = jnp.floor((site + 0.5) * (1.0 / LXY))
    site_x = site - site_y * LXY

    def spread_scalar(value):
        return jnp.full((1, LANES), value, jnp.int32)

    picked = []
    for o in range(4):
        choice = spread_scalar(pick[o])
        row = [jnp.zeros((1, LANES), jnp.int32)] * 3
        for r in range(table.shape[1]):
            row = [jnp.where(choice == r, spread_scalar(table[axis, r]), row[axis]) for axis in range(3)]
        picked.append(row)

    def path_momentum(path, axis):
        total = jnp.zeros((1, LANES), jnp.int32)
        for o in range(4):
            total = jnp.where(spread_scalar(dirs[o]) == path, picked[o][axis], total)
        return total.astype(F32)

    mom = [[path_momentum(path, axis) for axis in range(3)] for path in range(4)]
    extent_z = 1.0 * n_space
    plane = me.astype(F32)
    for slot, path, back in ((0, 0, (0, 0, 0)), (1, 1, (1, 0, 0)), (2, 2, (0, 1, 0)),
                             (3, 3, (0, 0, 0)), (4, 3, (0, 0, 1))):
        flat = 2.0 * math.pi * (mom[path][0] * (site_x - back[0]) / LXY
                                + mom[path][1] * (site_y - back[1]) / LXY
                                + mom[path][2] * (plane - back[2]) / extent_z)
        ph[slot, 0] = jnp.cos(flat)
        ph[slot, 1] = jnp.sin(flat)

    wait_bytes(lk, local_sem.at[1])
    flat_x = lax.rem(lax.broadcasted_iota(jnp.int32, (2, BLOCKS * LANES), 1), LXY)
    for d in range(3):
        for c in range(3):
            for a in range(3):
                pair = lk[d, c, a].astype(F32)
                if d == 0:
                    pair = jnp.where(flat_x == 0, pltpu.roll(pair, BLOCKS * LANES - LXY + 1, 1),
                                     pltpu.roll(pair, 1, 1))
                elif d == 1:
                    pair = pltpu.roll(pair, LXY, 1)
                at = (c * 3 + a) * 2
                lkf[d, at:at + 2, :] = pair
    wait_bytes(vbuf, local_sem.at[0])

    acc[...] = jnp.zeros_like(acc)
    accz[...] = jnp.zeros_like(accz)
    lane = lax.broadcasted_iota(jnp.int32, (16, LANES), 1)

    def link_rows(ref, at):
        return [[[jnp.broadcast_to(ref[pl.ds((c * 3 + a) * 2 + ri, 1), at], (8, LANES))
                  for a in range(3)] for c in range(3)] for ri in range(2)]

    def back_block(load, u, slot, j, dst, row, col):
        cosine = jnp.broadcast_to(ph[slot, 0, pl.ds(j, 1), :], (8, LANES))
        sine = jnp.broadcast_to(ph[slot, 1, pl.ds(j, 1), :], (8, LANES))

        def tile(k, carry):
            at = pl.multiple_of(k * 16, 16)
            v = [[load(ri, c, pl.ds(at, 16)) for c in range(3)] for ri in range(2)]
            for a in range(3):
                halves = []
                for h in range(2):
                    w = [[v[ri][c][h * 8:h * 8 + 8] for c in range(3)] for ri in range(2)]
                    b_re = u[0][0][a] * w[0][0] + u[1][0][a] * w[1][0]
                    b_im = u[0][0][a] * w[1][0] - u[1][0][a] * w[0][0]
                    for c in (1, 2):
                        b_re = b_re + u[0][c][a] * w[0][c] + u[1][c][a] * w[1][c]
                        b_im = b_im + u[0][c][a] * w[1][c] - u[1][c][a] * w[0][c]
                    halves.append((cosine * b_re, cosine * b_im, sine * b_re, sine * b_im))
                lanes = pl.ds((col * 3 + a) * LANES, LANES)
                for i in range(4):
                    dst[pl.ds(at + row + i * 128, 16), lanes] = jnp.concatenate(
                        [halves[0][i], halves[1][i]], axis=0).astype(BF16)
            return carry

        lax.fori_loop(0, NV // 16, tile, 0, unroll=True)

    def plain_block(j, dst, col):
        cosine = jnp.broadcast_to(ph[0, 0, pl.ds(j, 1), :], (16, LANES))
        sine = jnp.broadcast_to(ph[0, 1, pl.ds(j, 1), :], (16, LANES))

        def tile(k, carry):
            at = pl.multiple_of(k * 16, 16)
            for c in range(3):
                v_re = vbuf[j, 0, c, pl.ds(at, 16), :].astype(F32)
                v_im = vbuf[j, 1, c, pl.ds(at, 16), :].astype(F32)
                lanes = pl.ds((col * 3 + c) * LANES, LANES)
                dst[pl.ds(at, 16), lanes] = (cosine * v_re + sine * v_im).astype(BF16)
                dst[pl.ds(at + 128, 16), lanes] = (cosine * v_im - sine * v_re).astype(BF16)
            return carry

        lax.fori_loop(0, NV // 16, tile, 0, unroll=True)

    def stacked(parts):
        return jnp.concatenate(
            [jnp.concatenate([p[ri, c] for p in parts for c in range(3)], axis=1) for ri in range(2)],
            axis=0)

    def fill(i, dst):
        for s in range(2):
            j = 2 * i + s
            after = jnp.where(j == BLOCKS - 1, 0, j + 1)
            before = jnp.where(j == 0, BLOCKS - 1, j - 1)
            at = pl.ds(pl.multiple_of(j * LANES, LANES), LANES)
            plain_block(j, dst, s)
            first = lax.rem(j * LANES + lane, LXY) == 0

            def from_x(ri, c, rows):
                here = vbuf[j, ri, c, rows, :].astype(F32)
                near = jnp.where(lane == LANES - 1, vbuf[before, ri, c, rows, :].astype(F32), here)
                far = jnp.where(lane < LXY - 1, vbuf[after, ri, c, rows, :].astype(F32), here)
                return jnp.where(first, pltpu.roll(far, LANES - LXY + 1, 1), pltpu.roll(near, 1, 1))

            def from_y(ri, c, rows):
                return pltpu.roll(jnp.where(lane >= LANES - LXY, vbuf[before, ri, c, rows, :].astype(F32),
                                            vbuf[j, ri, c, rows, :].astype(F32)), LXY, 1)

            back_block(from_x, link_rows(lkf.at[0], at), 1, j, dst, 256, s)
            back_block(from_y, link_rows(lkf.at[1], at), 2, j, dst, 768, s)

    def add_dot(i, src):
        acc[...] += dot_nt(src[...], stacked([vbuf.at[2 * i], vbuf.at[2 * i + 1]]))

    def two_pairs(i, carry):
        fill(2 * i, lhs)
        add_dot(jnp.maximum(2 * i - 1, 0), lhs2)
        fill(2 * i + 1, lhs2)
        add_dot(2 * i, lhs)
        return carry

    lhs2[...] = jnp.zeros_like(lhs2)
    lax.fori_loop(0, BLOCKS // 4, two_pairs, 0)
    fill(BLOCKS // 2 - 1, lhs)
    add_dot(BLOCKS // 2 - 2, lhs2)
    add_dot(BLOCKS // 2 - 1, lhs)

    def blocks_of(ref, row):
        g_rr = ref[row:row + 128, 0:128]
        g_ri = ref[row:row + 128, 128:256]
        g_ir = ref[row + 128:row + 256, 0:128]
        g_ii = ref[row + 128:row + 256, 128:256]
        return g_rr + g_ii, g_ri - g_ir

    def finish_direction(d):
        sums, row = (accz, 0) if d == 2 else (acc, 256 + 512 * d)
        c_re, c_im = blocks_of(sums, row)
        s_re, s_im = blocks_of(sums, row + 256)
        length = (float(LXY), float(LXY), extent_z)[d]
        turn = jnp.full((1, LANES), 2.0 * math.pi / length, F32) * mom[d + 1][d]
        cosine = jnp.cos(turn)
        sine = jnp.sin(turn)
        p_re = c_re - s_im
        p_im = c_im + s_re
        n_re = cosine * p_re - sine * p_im
        n_im = sine * p_re + cosine * p_im
        part[d + 1, 0] = c_re + s_im - n_re.T
        part[d + 1, 1] = c_im - s_re + n_im.T

    plain_re, plain_im = blocks_of(acc, 0)
    part[0, 0] = plain_re.T
    part[0, 1] = -plain_im.T
    finish_direction(0)
    finish_direction(1)

    def spread(first, count, which):
        width = 16 * count
        for j in range(n_space):
            for p in range(count):
                for ri in range(2):
                    own[which, pl.ds(p * 16 + ri * 8, 8), :] = part[first + p, ri, j * 8:(j + 1) * 8, :]
            rs_send[which, j, 0:width, :] = own[which, 0:width, :].astype(BF16)
        for p in range(count):
            for ri in range(2):
                own[which, pl.ds(p * 16 + ri * 8, 8), :] = part[
                    first + p, ri, pl.ds(pl.multiple_of(me * 8, 8), 8), :]

        def send(k, carry):
            j = lax.rem(me + k, n_space)
            remote(rs_send.at[which, j, pl.ds(0, width)], rs_recv.at[which, k - 1, pl.ds(0, width)],
                   rs_sem.at[which, 0], rs_sem.at[which, 1], dev(t, j)).start()
            return carry

        lax.fori_loop(1, n_space, send, 0)

    def gather(which, width):
        wait_bytes(rs_recv.at[which, :, pl.ds(0, width)], rs_sem.at[which, 1])
        total = own[which, 0:width, :]
        for k in range(n_space - 1):
            total = total + rs_recv[which, k, 0:width, :].astype(F32)
        own[which, 0:width, :] = total

    def publish(which, width):
        ag_send[which, 0:width, :] = own[which, 0:width, :].astype(BF16)

        def send(j, carry):
            remote(ag_send.at[which, pl.ds(0, width)], ag.at[which, 0, me, pl.ds(0, width)],
                   ag_sem.at[which, 0], ag_sem.at[which, 1], dev(t_next, j)).start()
            remote(ag_send.at[which, pl.ds(0, width)], ag.at[which, 1, me, pl.ds(0, width)],
                   ag_sem.at[which, 0], ag_sem.at[which, 1], dev(t_prev, j)).start()
            return carry

        lax.fori_loop(0, n_space, send, 0)

    spread(0, 3, 0)

    link_copy.wait()
    for c in range(3):
        for a in range(3):
            at = (c * 3 + a) * 2
            lkupf[at:at + 2, :] = lkup[c, a].astype(F32)

    def z_block(n, carry):
        halo(n, 0).wait_recv()
        halo(n, 1).wait_recv()
        at = pl.ds(pl.multiple_of(n * LANES, LANES), LANES)
        m = n + HALF
        back_block(lambda ri, c, rows: vbuf[n, ri, c, rows, :].astype(F32), link_rows(lkf.at[2], at), 3, n, lhsz, 0, 0)
        back_block(lambda ri, c, rows: rup[n, ri, c, rows, :].astype(F32), link_rows(lkupf, at), 4, m, lhsz, 0, 1)
        accz[...] += dot_nt(lhsz[...], stacked([rdn.at[n], vbuf.at[m]]))
        return carry

    def wait_halo_sends(lo, hi):
        def one(n, carry):
            halo(n, 0).wait_send()
            halo(n, 1).wait_send()
            return carry

        lax.fori_loop(lo, hi, one, 0)

    def weights(kind, e, which, count, first_path):
        src = e if kind == 0 else 1 - e
        rows = []
        for p in range(count):
            both = [ag[which, src, j, pl.ds(p * 16, 16), :].astype(F32) for j in range(n_space)]
            phi_re = jnp.concatenate([x[0:8] for x in both], axis=0)
            phi_im = jnp.concatenate([x[8:16] for x in both], axis=0)
            if kind == 0:
                rows += [jnp.concatenate([phi_re, phi_im], axis=1), jnp.concatenate([phi_im, -phi_re], axis=1)]
            else:
                rows += [jnp.concatenate([phi_re, -phi_im], axis=1), jnp.concatenate([phi_im, phi_re], axis=1)]
        phi = jnp.concatenate(rows, axis=0).astype(BF16)
        mat = tauo.at[e] if kind == 0 else taun.at[e]
        for c in range(4):
            col = slice(c * 128, (c + 1) * 128)
            z = dot_nt(jnp.concatenate([mat[0, :, col], mat[1, :, col]], axis=1), phi)
            if kind == 1 and c >= 2:
                z = -z
            z = z.astype(BF16)
            for r in range(4):
                for p in range(2 * count):
                    zbuf[r, p * 128:(p + 1) * 128, col] = z[r * 128:(r + 1) * 128, p * 128:(p + 1) * 128]
        total = None
        for r in range(4):
            row = slice(r * 128, (r + 1) * 128)
            g = dot_nt(zbuf[r, 0:256 * count, :], jnp.concatenate([mat[0, row, :], mat[1, row, :]], axis=0))
            if total is None:
                total = g
            elif kind == 0 and r >= 2:
                total = total - g
            else:
                total = total + g
        for p in range(count):
            one = total[p * 256:(p + 1) * 256]
            rr, ri_, ir, ii = one[0:128, 0:128], one[0:128, 128:256], one[128:256, 0:128], one[128:256, 128:256]
            if kind == 0:
                wmat[kind, e, first_path + p, 0] = rr - ii
                wmat[kind, e, first_path + p, 1] = ri_ + ir
            else:
                wmat[kind, e, first_path + p, 0] = rr + ii
                wmat[kind, e, first_path + p, 1] = ir - ri_

    def weights_of(which, count, first_path):
        for kind in range(2):
            for e in range(2):
                weights(kind, e, which, count, first_path)

    def pair_rows(paths, lo, hi):
        for kind in range(2):
            for e in range(2):
                for p in paths:
                    def one(w, carry, kind=kind, e=e, p=p):
                        w_re, w_im = wmat[kind, e, w, 0], wmat[kind, e, w, 1]
                        p_re, p_im = part[p, 0], part[p, 1]
                        re = jnp.sum(p_re * w_re - p_im * w_im, axis=0, keepdims=True)
                        im = jnp.sum(p_re * w_im + p_im * w_re, axis=0, keepdims=True)
                        if kind == 0:
                            rowbuf[kind, w, pl.ds(e * 4 + p, 1), :] = re
                            rowbuf[kind, w, pl.ds(8 + e * 4 + p, 1), :] = im
                        else:
                            rowbuf[kind, p, pl.ds(e * 4 + w, 1), :] = re
                            rowbuf[kind, p, pl.ds(8 + e * 4 + w, 1), :] = im
                        return carry

                    lax.fori_loop(lo, hi, one, 0)

    def write_elementals():
        for o in range(4):
            path = jnp.full((8, LANES), dirs[o], jnp.int32)
            for ri in range(2):
                rows = own[1, ri * 8:(ri + 1) * 8, :]
                for p in range(3):
                    rows = jnp.where(path == p, own[0, p * 16 + ri * 8:p * 16 + ri * 8 + 8, :], rows)
                elem_out[o, ri, 0] = rows

    def write_correlators(total):
        col = lax.broadcasted_iota(jnp.int32, (16, LANES), 1)
        turned = jnp.zeros((16, LANES), F32)
        for q in range(4):
            one = jnp.sum(jnp.where(col == spread_scalar(dirs[q]), total, 0.0), axis=1, keepdims=True)
            turned = jnp.where(col == q, one, turned)
        for o in range(4):
            path = jnp.full((1, LANES), dirs[o], jnp.int32)
            for ri in range(2):
                for e in range(2):
                    at = ri * 8 + e * 4
                    row = turned[at:at + 1]
                    for p in range(1, 4):
                        row = jnp.where(path == p, turned[at + p:at + p + 1], row)
                    corr_out[ri, 0, e, o:o + 1, :] = row[:, 0:4]

    @pl.when(even)
    def _():
        lax.fori_loop(0, HALF - 2, z_block, 0)
        wait_halo_sends(0, HALF - 1)
        pl.semaphore_signal(go_sem, inc=1, device_id=dev(t_next, me), device_id_type=MESH)
        gather(0, 48)
        publish(0, 48)
        lax.fori_loop(HALF - 2, HALF, z_block, 0)
        finish_direction(2)
        spread(3, 1, 1)
        gather(1, 16)
        publish(1, 16)
        write_elementals()
        wait_halo_sends(HALF - 1, HALF)
        wait_bytes(taun.at[0], tau_sem.at[0])
        wait_bytes(taun.at[1], tau_sem.at[1])
        wait_bytes(rs_recv.at[0, :, pl.ds(0, 48)], rs_sem.at[0, 0])
        wait_bytes(rs_recv.at[1, :, pl.ds(0, 16)], rs_sem.at[1, 0])
        wait_bytes(ag.at[0, :, :, pl.ds(0, 48)], ag_sem.at[0, 0])
        wait_bytes(ag.at[1, :, :, pl.ds(0, 16)], ag_sem.at[1, 0])
        wait_bytes(ps_even, ps_sem.at[2])
        row = lax.broadcasted_iota(jnp.int32, (16, LANES), 0)
        first = ps_even[0, 0]
        second = ps_even[1, 0]
        for j in range(1, n_space):
            first = first + ps_even[0, j]
            second = second + ps_even[1, j]
        write_correlators(jnp.where(lax.rem(row, 8) < 4, first, second))

    @pl.when(odd)
    def _():
        pl.semaphore_wait(go_sem, 1)
        lax.fori_loop(0, HALF, start_halo, 0)
        gather(0, 48)
        lax.fori_loop(0, 2, z_block, 0)
        wait_bytes(taun.at[0], tau_sem.at[2])
        wait_bytes(taun.at[1], tau_sem.at[3])
        wait_bytes(tauo, local_sem.at[2])
        for e in range(2):
            for ri in range(2):
                taun[e, ri] = taun[e, ri].T
        wait_bytes(ag.at[0, :, :, pl.ds(0, 48)], ag_sem.at[0, 1])
        weights_of(0, 3, 0)
        lax.fori_loop(2, 5, z_block, 0)
        pair_rows((0, 1, 2), 0, 3)
        lax.fori_loop(5, HALF - 1, z_block, 0)
        wait_bytes(ag.at[1, :, :, pl.ds(0, 16)], ag_sem.at[1, 1])
        weights_of(1, 1, 3)
        pair_rows((0, 1, 2), 3, 4)
        lax.fori_loop(HALF - 1, HALF, z_block, 0)
        finish_direction(2)
        spread(3, 1, 1)
        pair_rows((3,), 0, 4)
        col = lax.broadcasted_iota(jnp.int32, (16, LANES), 1)
        for kind in range(2):
            tile = jnp.zeros((16, LANES), F32)
            for q in range(4):
                tile = jnp.where(col == q, jnp.sum(rowbuf[kind, q], axis=1, keepdims=True), tile)
            ps_send[kind] = tile

        def send_group(k, carry):
            remote(ps_send.at[0], ps_own.at[k - 1], ps_sem.at[0], ps_sem.at[1],
                   dev(t, lax.rem(me + k, n_space))).start()
            return carry

        def send_near(j, carry):
            remote(ps_send.at[1], ps_even.at[0, me], ps_sem.at[3], ps_sem.at[2], dev(t_next, j)).start()
            remote(ps_send.at[1], ps_even.at[1, me], ps_sem.at[3], ps_sem.at[2], dev(t_prev, j)).start()
            return carry

        lax.fori_loop(1, n_space, send_group, 0)
        lax.fori_loop(0, n_space, send_near, 0)
        gather(1, 16)
        write_elementals()
        wait_halo_sends(0, HALF)
        wait_bytes(rs_recv.at[0, :, pl.ds(0, 48)], rs_sem.at[0, 0])
        wait_bytes(rs_recv.at[1, :, pl.ds(0, 16)], rs_sem.at[1, 0])
        wait_bytes(ps_own, ps_sem.at[1])
        total = ps_send[0]
        for k in range(n_space - 1):
            total = total + ps_own[k]
        wait_bytes(ps_own, ps_sem.at[0])
        wait_bytes(ps_even, ps_sem.at[3])
        write_correlators(total)

    @pl.when(even)
    def _():
        wait_bytes(tauo, local_sem.at[2])


def solution(mesh):
    n_tm, n_space = mesh.shape["tm"], mesh.shape["space"]
    placed = (
        P("tm", None, None, None, "space"),
        P("tm", None, None, None, None, "space"),
        P("tm", None, None, None, None),
        P(),
        P(),
        P(),
    )

    def body(eigvecs, links, perambulators, directions, mom_pick, mom_table):
        hbm = pl.BlockSpec(memory_space=pl.ANY)
        smem = pl.BlockSpec(memory_space=pltpu.SMEM)
        vmem = pl.BlockSpec(memory_space=pltpu.VMEM)
        dma = pltpu.SemaphoreType.DMA
        return pl.pallas_call(
            functools.partial(kernel, n_tm, n_space),
            out_shape=(
                jax.ShapeDtypeStruct((4, 2, 1, ROWS, NV), F32),
                jax.ShapeDtypeStruct((2, 1, 2, 4, 4), F32),
            ),
            in_specs=[hbm, hbm, hbm, smem, smem, smem],
            out_specs=(vmem, vmem),
            scratch_shapes=[
                pltpu.VMEM((BLOCKS, 2, 3, NV, LANES), BF16),
                pltpu.VMEM((HALF, 2, 3, NV, LANES), BF16),
                pltpu.VMEM((HALF, 2, 3, NV, LANES), BF16),
                pltpu.VMEM((3, 3, 3, 2, BLOCKS * LANES), BF16),
                pltpu.VMEM((3, 3, 2, HALF * LANES), BF16),
                pltpu.VMEM((3, 24, BLOCKS * LANES), F32),
                pltpu.VMEM((24, HALF * LANES), F32),
                pltpu.VMEM((5, 2, 24, LANES), F32),
                pltpu.VMEM((1280, 768), BF16),
                pltpu.VMEM((1280, 768), BF16),
                pltpu.VMEM((512, 768), BF16),
                pltpu.VMEM((1280, 256), F32),
                pltpu.VMEM((512, 256), F32),
                pltpu.VMEM((4, 2, NV, NV), F32),
                pltpu.VMEM((2, n_space, 48, NV), BF16),
                pltpu.VMEM((2, n_space - 1, 48, NV), BF16),
                pltpu.VMEM((2, 48, NV), F32),
                pltpu.VMEM((2, 48, NV), BF16),
                pltpu.VMEM((2, 2, n_space, 48, NV), BF16),
                pltpu.VMEM((2, 2, 512, 512), BF16),
                pltpu.VMEM((2, 2, 512, 512), BF16),
                pltpu.VMEM((4, 768, 512), BF16),
                pltpu.VMEM((2, 2, 4, 2, NV, NV), F32),
                pltpu.VMEM((2, 4, 16, NV), F32),
                pltpu.VMEM((2, 16, NV), F32),
                pltpu.VMEM((n_space - 1, 16, NV), F32),
                pltpu.VMEM((2, n_space, 16, NV), F32),
                dma((3,)),
                dma((2, HALF)),
                dma((2, HALF)),
                dma((2,)),
                dma((4,)),
                dma((2, 2)),
                dma((2, 2)),
                dma((4,)),
                pltpu.SemaphoreType.REGULAR,
            ],
            compiler_params=pltpu.CompilerParams(
                collective_id=0, has_side_effects=True, vmem_limit_bytes=60 << 20),
            name="elementals_and_correlators",
        )(eigvecs, jnp.transpose(links, (0, 1, 3, 4, 2, 5)), perambulators, directions, mom_pick,
          mom_table.T)

    return jax.shard_map(
        body,
        mesh=mesh,
        in_specs=placed,
        out_specs=(P(None, None, "tm", "space", None), P(None, "tm", None, None, None)),
        check_vma=False,
    )
```

```python
import functools
import math

import jax
import jax.numpy as jnp
from jax import lax
from jax.experimental import pallas as pl
from jax.experimental.pallas import tpu as pltpu
from jax.sharding import PartitionSpec as P

LXY = 48
MESH = pl.DeviceIdType.MESH
F32 = jnp.float32
BF16 = jnp.bfloat16
NT = (((1,), (1,)), ((), ()))
LANES = 128
HALF = 9
BLOCKS = 18
NV = 128
ROWS = 8


def dot_nt(a, b):
    return lax.dot_general(a, b, NT, preferred_element_type=F32)


def kernel(n_tm, n_space, eig, links, tau, dirs, pick, table, elem_out, corr_out,
           vbuf, rdn, rup, lk, lkup, lkf, lkupf, ph, lhs, lhs2, lhsz, acc, accz, part,
           rs_send, rs_recv, own, ag_send, ag, tauo, taun, zbuf, wmat, rowbuf,
           ysend, yrecv, ps_send, ps_own, ps_even, local_sem, halo_send, halo_recv, lk_sem,
           rs_sem, ag_sem, fw_sem, y_sem, ps_sem, go_sem):
    t = lax.axis_index("tm")
    me = lax.axis_index("space")
    odd = lax.rem(t, 2) == 1
    even = lax.rem(t, 2) == 0
    t_next = lax.rem(t + 1, n_tm)
    t_prev = lax.rem(t + n_tm - 1, n_tm)
    up = lax.rem(me + 1, n_space)
    down = lax.rem(me + n_space - 1, n_space)

    def dev(a, b):
        return {"tm": a, "space": b}

    def remote(src, dst, ssem, rsem, where):
        return pltpu.make_async_remote_copy(
            src_ref=src, dst_ref=dst, send_sem=ssem, recv_sem=rsem,
            device_id=where, device_id_type=MESH)

    def wait_bytes(ref, sem):
        pltpu.make_async_copy(ref, ref, sem).wait()

    def load_block(j):
        return pltpu.make_async_copy(
            eig.at[0, :, :, :, pl.ds(pl.multiple_of(j * LANES, LANES), LANES)],
            vbuf.at[j], local_sem.at[0])

    pltpu.make_async_copy(links.at[0], lk, local_sem.at[1]).start()

    def start_load(j, carry):
        load_block(j).start()
        return carry

    lax.fori_loop(0, BLOCKS, start_load, 0)
    pltpu.make_async_copy(tau.at[0], tauo, local_sem.at[2]).start()

    barrier = pltpu.get_barrier_semaphore()

    def greet(a, b):
        pl.semaphore_signal(barrier, inc=1, device_id=dev(a, b), device_id_type=MESH)

    greet(t, up)
    greet(t, down)

    def greet_group(k, carry):
        greet(t, lax.rem(me + k, n_space))
        return carry

    lax.fori_loop(2, n_space - 1, greet_group, 0)

    def greet_near(k, carry):
        greet(t_next, k)
        greet(t_prev, k)
        return carry

    lax.fori_loop(0, n_space, greet_near, 0)
    pl.semaphore_wait(barrier, 3 * n_space - 1)

    def halo(n, side):
        j = n + HALF * side
        return remote(
            eig.at[0, :, :, :, pl.ds(pl.multiple_of(j * LANES, LANES), LANES)],
            (rup if side else rdn).at[n], halo_send.at[side, n], halo_recv.at[side, n],
            dev(t, up if side else down))

    def start_halo(n, carry):
        halo(n, 0).start()
        halo(n, 1).start()
        return carry

    link_copy = remote(links.at[0, 2, :, :, :, pl.ds(HALF * LANES, HALF * LANES)], lkup,
                       lk_sem.at[0], lk_sem.at[1], dev(t, up))
    link_copy.start()

    @pl.when(even)
    def _():
        lax.fori_loop(0, HALF, start_halo, 0)

    site = (lax.broadcasted_iota(jnp.int32, (24, LANES), 0) * LANES
            + lax.broadcasted_iota(jnp.int32, (24, LANES), 1)).astype(F32)
    site_y = jnp.floor((site + 0.5) * (1.0 / LXY))
    site_x = site - site_y * LXY

    def spread_scalar(value):
        return jnp.full((1, LANES), value, jnp.int32)

    picked = []
    for o in range(4):
        choice = spread_scalar(pick[o])
        row = [jnp.zeros((1, LANES), jnp.int32)] * 3
        for r in range(table.shape[1]):
            row = [jnp.where(choice == r, spread_scalar(table[axis, r]), row[axis]) for axis in range(3)]
        picked.append(row)

    def path_momentum(path, axis):
        total = jnp.zeros((1, LANES), jnp.int32)
        for o in range(4):
            total = jnp.where(spread_scalar(dirs[o]) == path, picked[o][axis], total)
        return total.astype(F32)

    mom = [[path_momentum(path, axis) for axis in range(3)] for path in range(4)]
    extent_z = 1.0 * n_space
    plane = me.astype(F32)
    for slot, path, back in ((0, 0, (0, 0, 0)), (1, 1, (1, 0, 0)), (2, 2, (0, 1, 0)),
                             (3, 3, (0, 0, 0)), (4, 3, (0, 0, 1))):
        flat = 2.0 * math.pi * (mom[path][0] * (site_x - back[0]) / LXY
                                + mom[path][1] * (site_y - back[1]) / LXY
                                + mom[path][2] * (plane - back[2]) / extent_z)
        ph[slot, 0] = jnp.cos(flat)
        ph[slot, 1] = jnp.sin(flat)

    wait_bytes(lk, local_sem.at[1])
    flat_x = lax.rem(lax.broadcasted_iota(jnp.int32, (2, BLOCKS * LANES), 1), LXY)
    for d in range(3):
        for c in range(3):
            for a in range(3):
                pair = lk[d, c, a].astype(F32)
                if d == 0:
                    pair = jnp.where(flat_x == 0, pltpu.roll(pair, BLOCKS * LANES - LXY + 1, 1),
                                     pltpu.roll(pair, 1, 1))
                elif d == 1:
                    pair = pltpu.roll(pair, LXY, 1)
                at = (c * 3 + a) * 2
                lkf[d, at:at + 2, :] = pair
    wait_bytes(vbuf, local_sem.at[0])

    acc[...] = jnp.zeros_like(acc)
    accz[...] = jnp.zeros_like(accz)
    lane = lax.broadcasted_iota(jnp.int32, (16, LANES), 1)

    def link_rows(ref, at):
        return [[[jnp.broadcast_to(ref[pl.ds((c * 3 + a) * 2 + ri, 1), at], (8, LANES))
                  for a in range(3)] for c in range(3)] for ri in range(2)]

    def back_block(load, u, slot, j, dst, row, col):
        cosine = jnp.broadcast_to(ph[slot, 0, pl.ds(j, 1), :], (8, LANES))
        sine = jnp.broadcast_to(ph[slot, 1, pl.ds(j, 1), :], (8, LANES))

        def tile(k, carry):
            at = pl.multiple_of(k * 16, 16)
            v = [[load(ri, c, pl.ds(at, 16)) for c in range(3)] for ri in range(2)]
            for a in range(3):
                halves = []
                for h in range(2):
                    w = [[v[ri][c][h * 8:h * 8 + 8] for c in range(3)] for ri in range(2)]
                    b_re = u[0][0][a] * w[0][0] + u[1][0][a] * w[1][0]
                    b_im = u[0][0][a] * w[1][0] - u[1][0][a] * w[0][0]
                    for c in (1, 2):
                        b_re = b_re + u[0][c][a] * w[0][c] + u[1][c][a] * w[1][c]
                        b_im = b_im + u[0][c][a] * w[1][c] - u[1][c][a] * w[0][c]
                    halves.append((cosine * b_re, cosine * b_im, sine * b_re, sine * b_im))
                lanes = pl.ds((col * 3 + a) * LANES, LANES)
                for i in range(4):
                    dst[pl.ds(at + row + i * 128, 16), lanes] = jnp.concatenate(
                        [halves[0][i], halves[1][i]], axis=0).astype(BF16)
            return carry

        lax.fori_loop(0, NV // 16, tile, 0, unroll=True)

    def plain_block(j, dst, col):
        cosine = jnp.broadcast_to(ph[0, 0, pl.ds(j, 1), :], (16, LANES))
        sine = jnp.broadcast_to(ph[0, 1, pl.ds(j, 1), :], (16, LANES))

        def tile(k, carry):
            at = pl.multiple_of(k * 16, 16)
            for c in range(3):
                v_re = vbuf[j, 0, c, pl.ds(at, 16), :].astype(F32)
                v_im = vbuf[j, 1, c, pl.ds(at, 16), :].astype(F32)
                lanes = pl.ds((col * 3 + c) * LANES, LANES)
                dst[pl.ds(at, 16), lanes] = (cosine * v_re + sine * v_im).astype(BF16)
                dst[pl.ds(at + 128, 16), lanes] = (cosine * v_im - sine * v_re).astype(BF16)
            return carry

        lax.fori_loop(0, NV // 16, tile, 0, unroll=True)

    def stacked(parts):
        return jnp.concatenate(
            [jnp.concatenate([p[ri, c] for p in parts for c in range(3)], axis=1) for ri in range(2)],
            axis=0)

    def fill(i, dst):
        for s in range(2):
            j = 2 * i + s
            after = jnp.where(j == BLOCKS - 1, 0, j + 1)
            before = jnp.where(j == 0, BLOCKS - 1, j - 1)
            at = pl.ds(pl.multiple_of(j * LANES, LANES), LANES)
            plain_block(j, dst, s)
            first = lax.rem(j * LANES + lane, LXY) == 0

            def from_x(ri, c, rows):
                here = vbuf[j, ri, c, rows, :].astype(F32)
                near = jnp.where(lane == LANES - 1, vbuf[before, ri, c, rows, :].astype(F32), here)
                far = jnp.where(lane < LXY - 1, vbuf[after, ri, c, rows, :].astype(F32), here)
                return jnp.where(first, pltpu.roll(far, LANES - LXY + 1, 1), pltpu.roll(near, 1, 1))

            def from_y(ri, c, rows):
                return pltpu.roll(jnp.where(lane >= LANES - LXY, vbuf[before, ri, c, rows, :].astype(F32),
                                            vbuf[j, ri, c, rows, :].astype(F32)), LXY, 1)

            back_block(from_x, link_rows(lkf.at[0], at), 1, j, dst, 256, s)
            back_block(from_y, link_rows(lkf.at[1], at), 2, j, dst, 768, s)

    def add_dot(i, src):
        acc[...] += dot_nt(src[...], stacked([vbuf.at[2 * i], vbuf.at[2 * i + 1]]))

    def two_pairs(i, carry):
        fill(2 * i, lhs)
        add_dot(jnp.maximum(2 * i - 1, 0), lhs2)
        fill(2 * i + 1, lhs2)
        add_dot(2 * i, lhs)
        return carry

    lhs2[...] = jnp.zeros_like(lhs2)
    lax.fori_loop(0, BLOCKS // 4, two_pairs, 0)
    fill(BLOCKS // 2 - 1, lhs)
    add_dot(BLOCKS // 2 - 2, lhs2)
    add_dot(BLOCKS // 2 - 1, lhs)

    def blocks_of(ref, row):
        g_rr = ref[row:row + 128, 0:128]
        g_ri = ref[row:row + 128, 128:256]
        g_ir = ref[row + 128:row + 256, 0:128]
        g_ii = ref[row + 128:row + 256, 128:256]
        return g_rr + g_ii, g_ri - g_ir

    def finish_direction(d):
        sums, row = (accz, 0) if d == 2 else (acc, 256 + 512 * d)
        c_re, c_im = blocks_of(sums, row)
        s_re, s_im = blocks_of(sums, row + 256)
        length = (float(LXY), float(LXY), extent_z)[d]
        turn = jnp.full((1, LANES), 2.0 * math.pi / length, F32) * mom[d + 1][d]
        cosine = jnp.cos(turn)
        sine = jnp.sin(turn)
        p_re = c_re - s_im
        p_im = c_im + s_re
        n_re = cosine * p_re - sine * p_im
        n_im = sine * p_re + cosine * p_im
        part[d + 1, 0] = c_re + s_im - n_re.T
        part[d + 1, 1] = c_im - s_re + n_im.T

    plain_re, plain_im = blocks_of(acc, 0)
    part[0, 0] = plain_re.T
    part[0, 1] = -plain_im.T
    finish_direction(0)
    finish_direction(1)

    def spread(first, count, which):
        width = 16 * count
        for j in range(n_space):
            for p in range(count):
                for ri in range(2):
                    own[which, pl.ds(p * 16 + ri * 8, 8), :] = part[first + p, ri, j * 8:(j + 1) * 8, :]
            rs_send[which, j, 0:width, :] = own[which, 0:width, :].astype(BF16)
        for p in range(count):
            for ri in range(2):
                own[which, pl.ds(p * 16 + ri * 8, 8), :] = part[
                    first + p, ri, pl.ds(pl.multiple_of(me * 8, 8), 8), :]

        def send(k, carry):
            j = lax.rem(me + k, n_space)
            remote(rs_send.at[which, j, pl.ds(0, width)], rs_recv.at[which, k - 1, pl.ds(0, width)],
                   rs_sem.at[which, 0], rs_sem.at[which, 1], dev(t, j)).start()
            return carry

        lax.fori_loop(1, n_space, send, 0)

    def gather(which, width):
        wait_bytes(rs_recv.at[which, :, pl.ds(0, width)], rs_sem.at[which, 1])
        total = own[which, 0:width, :]
        for k in range(n_space - 1):
            total = total + rs_recv[which, k, 0:width, :].astype(F32)
        own[which, 0:width, :] = total

    def publish(which, width):
        ag_send[which, 0:width, :] = own[which, 0:width, :].astype(BF16)
        ag[which, 0, me, 0:width, :] = ag_send[which, 0:width, :]

        def send(k, carry):
            remote(ag_send.at[which, pl.ds(0, width)], ag.at[which, 0, me, pl.ds(0, width)],
                   ag_sem.at[which, 0], ag_sem.at[which, 1],
                   dev(t, lax.rem(me + k, n_space))).start()
            return carry

        lax.fori_loop(1, n_space, send, 0)

    def forward(which, width):
        wait_bytes(ag.at[which, 0, pl.ds(0, n_space - 1), pl.ds(0, width)], ag_sem.at[which, 1])
        for side, where in ((0, t_next), (1, t_prev)):
            remote(ag.at[which, 0, :, pl.ds(0, width)], ag.at[which, side, :, pl.ds(0, width)],
                   fw_sem.at[which, side], fw_sem.at[which, 2], dev(where, me)).start()

    def send_weights(which, first_path, count):
        for e, where in ((0, t_prev), (1, t_next)):
            paths = pl.ds(first_path, count)
            remote(ysend.at[e, paths], yrecv.at[e, paths], y_sem.at[which, 0, e], y_sem.at[which, 1, e],
                   dev(where, me)).start()

    def wait_weights(which, first_path, count, side):
        for e in range(2):
            wait_bytes(yrecv.at[e, pl.ds(first_path, count)], y_sem.at[which, side, e])

    @pl.when(even)
    def _():
        spread(0, 3, 0)


    link_copy.wait()
    for c in range(3):
        for a in range(3):
            at = (c * 3 + a) * 2
            lkupf[at:at + 2, :] = lkup[c, a].astype(F32)

    def z_block(n, carry):
        halo(n, 0).wait_recv()
        halo(n, 1).wait_recv()
        at = pl.ds(pl.multiple_of(n * LANES, LANES), LANES)
        m = n + HALF
        back_block(lambda ri, c, rows: vbuf[n, ri, c, rows, :].astype(F32), link_rows(lkf.at[2], at), 3, n, lhsz, 0, 0)
        back_block(lambda ri, c, rows: rup[n, ri, c, rows, :].astype(F32), link_rows(lkupf, at), 4, m, lhsz, 0, 1)
        accz[...] += dot_nt(lhsz[...], stacked([rdn.at[n], vbuf.at[m]]))
        return carry

    def wait_halo_sends(lo, hi):
        def one(n, carry):
            halo(n, 0).wait_send()
            halo(n, 1).wait_send()
            return carry

        lax.fori_loop(lo, hi, one, 0)

    def weights(kind, e, which, count, first_path):
        src = e if kind == 0 else 0
        rows = []
        for p in range(count):
            both = [ag[which, src, j, pl.ds(p * 16, 16), :].astype(F32) for j in range(n_space)]
            phi_re = jnp.concatenate([x[0:8] for x in both], axis=0)
            phi_im = jnp.concatenate([x[8:16] for x in both], axis=0)
            if kind == 0:
                rows += [jnp.concatenate([phi_re, phi_im], axis=1), jnp.concatenate([phi_im, -phi_re], axis=1)]
            else:
                rows += [jnp.concatenate([phi_re, -phi_im], axis=1), jnp.concatenate([phi_im, phi_re], axis=1)]
        phi = jnp.concatenate(rows, axis=0).astype(BF16)
        mat = tauo.at[e] if kind == 0 else taun.at[e]
        for c in range(4):
            col = slice(c * 128, (c + 1) * 128)
            z = dot_nt(jnp.concatenate([mat[0, :, col], mat[1, :, col]], axis=1), phi)
            if kind == 1 and c >= 2:
                z = -z
            z = z.astype(BF16)
            for r in range(4):
                for p in range(2 * count):
                    zbuf[r, p * 128:(p + 1) * 128, col] = z[r * 128:(r + 1) * 128, p * 128:(p + 1) * 128]
        total = None
        for r in range(4):
            row = slice(r * 128, (r + 1) * 128)
            g = dot_nt(zbuf[r, 0:256 * count, :], jnp.concatenate([mat[0, row, :], mat[1, row, :]], axis=0))
            if total is None:
                total = g
            elif kind == 0 and r >= 2:
                total = total - g
            else:
                total = total + g
        for p in range(count):
            one = total[p * 256:(p + 1) * 256]
            rr, ri_, ir, ii = one[0:128, 0:128], one[0:128, 128:256], one[128:256, 0:128], one[128:256, 128:256]
            if kind == 0:
                wmat[e, first_path + p, 0] = rr - ii
                wmat[e, first_path + p, 1] = ri_ + ir
            else:
                ysend[e, first_path + p, 0] = (rr + ii).astype(BF16)
                ysend[e, first_path + p, 1] = (ir - ri_).astype(BF16)

    def weights_of(kind, which, count, first_path):
        for e in range(2):
            weights(kind, e, which, count, first_path)

    def pair_rows(kind, paths, lo, hi):
        mat = wmat if kind == 0 else yrecv
        for e in range(2):
            for p in paths:
                def one(w, carry, e=e, p=p):
                    w_re, w_im = mat[e, w, 0].astype(F32), mat[e, w, 1].astype(F32)
                    p_re, p_im = part[p, 0], part[p, 1]
                    re = jnp.sum(p_re * w_re - p_im * w_im, axis=0, keepdims=True)
                    im = jnp.sum(p_re * w_im + p_im * w_re, axis=0, keepdims=True)
                    if kind == 0:
                        rowbuf[kind, w, pl.ds(e * 4 + p, 1), :] = re
                        rowbuf[kind, w, pl.ds(8 + e * 4 + p, 1), :] = im
                    else:
                        rowbuf[kind, p, pl.ds(e * 4 + w, 1), :] = re
                        rowbuf[kind, p, pl.ds(8 + e * 4 + w, 1), :] = im
                    return carry

                lax.fori_loop(lo, hi, one, 0)

    def write_elementals():
        for o in range(4):
            path = jnp.full((8, LANES), dirs[o], jnp.int32)
            for ri in range(2):
                rows = own[1, ri * 8:(ri + 1) * 8, :]
                for p in range(3):
                    rows = jnp.where(path == p, own[0, p * 16 + ri * 8:p * 16 + ri * 8 + 8, :], rows)
                elem_out[o, ri, 0] = rows

    def write_correlators(total):
        col = lax.broadcasted_iota(jnp.int32, (16, LANES), 1)
        turned = jnp.zeros((16, LANES), F32)
        for q in range(4):
            one = jnp.sum(jnp.where(col == spread_scalar(dirs[q]), total, 0.0), axis=1, keepdims=True)
            turned = jnp.where(col == q, one, turned)
        for o in range(4):
            path = jnp.full((1, LANES), dirs[o], jnp.int32)
            for ri in range(2):
                for e in range(2):
                    at = ri * 8 + e * 4
                    row = turned[at:at + 1]
                    for p in range(1, 4):
                        row = jnp.where(path == p, turned[at + p:at + p + 1], row)
                    corr_out[ri, 0, e, o:o + 1, :] = row[:, 0:4]

    @pl.when(even)
    def _():
        lax.fori_loop(0, 4, z_block, 0)
        wait_halo_sends(0, 5)
        pl.semaphore_signal(go_sem, inc=1, device_id=dev(t_next, me), device_id_type=MESH)
        lax.fori_loop(4, HALF, z_block, 0)
        finish_direction(2)
        spread(3, 1, 1)
        gather(0, 48)
        publish(0, 48)
        wait_bytes(tauo, local_sem.at[2])
        for e in range(2):
            for ri in range(2):
                taun[e, ri] = tauo[e, ri].T
        gather(1, 16)
        publish(1, 16)
        forward(0, 48)
        weights_of(1, 0, 3, 0)
        send_weights(0, 0, 3)
        forward(1, 16)
        weights_of(1, 1, 1, 3)
        send_weights(1, 3, 1)
        write_elementals()
        wait_halo_sends(5, HALF)
        wait_bytes(rs_recv.at[0, :, pl.ds(0, 48)], rs_sem.at[0, 0])
        wait_bytes(rs_recv.at[1, :, pl.ds(0, 16)], rs_sem.at[1, 0])
        for which, width in ((0, 48), (1, 16)):
            wait_bytes(ag.at[which, 0, pl.ds(0, n_space - 1), pl.ds(0, width)], ag_sem.at[which, 0])
            for side in range(2):
                wait_bytes(ag.at[which, 0, :, pl.ds(0, width)], fw_sem.at[which, side])
        wait_weights(0, 0, 3, 0)
        wait_weights(1, 3, 1, 0)
        wait_bytes(ps_even, ps_sem.at[2])
        row = lax.broadcasted_iota(jnp.int32, (16, LANES), 0)
        first = ps_even[0, 0]
        second = ps_even[1, 0]
        for j in range(1, n_space):
            first = first + ps_even[0, j]
            second = second + ps_even[1, j]
        write_correlators(jnp.where(lax.rem(row, 8) < 4, first, second))

    @pl.when(odd)
    def _():
        pl.semaphore_wait(go_sem, 1)
        lax.fori_loop(0, HALF, start_halo, 0)
        lax.fori_loop(0, 7, z_block, 0)
        wait_bytes(tauo, local_sem.at[2])
        wait_bytes(ag.at[0, :, :, pl.ds(0, 48)], fw_sem.at[0, 2])
        weights_of(0, 0, 3, 0)
        pair_rows(0, (0, 1, 2), 0, 3)
        lax.fori_loop(7, HALF, z_block, 0)
        finish_direction(2)
        spread(3, 1, 1)
        spread(0, 3, 0)
        pair_rows(0, (3,), 0, 3)
        wait_weights(0, 0, 3, 1)
        pair_rows(1, (0, 1, 2, 3), 0, 3)
        wait_bytes(ag.at[1, :, :, pl.ds(0, 16)], fw_sem.at[1, 2])
        weights_of(0, 1, 1, 3)
        pair_rows(0, (0, 1, 2, 3), 3, 4)
        wait_weights(1, 3, 1, 1)
        pair_rows(1, (0, 1, 2, 3), 3, 4)
        col = lax.broadcasted_iota(jnp.int32, (16, LANES), 1)
        for kind in range(2):
            tile = jnp.zeros((16, LANES), F32)
            for q in range(4):
                tile = jnp.where(col == q, jnp.sum(rowbuf[kind, q], axis=1, keepdims=True), tile)
            ps_send[kind] = tile

        def send_group(k, carry):
            remote(ps_send.at[0], ps_own.at[k - 1], ps_sem.at[0], ps_sem.at[1],
                   dev(t, lax.rem(me + k, n_space))).start()
            return carry

        def send_near(j, carry):
            remote(ps_send.at[1], ps_even.at[0, me], ps_sem.at[3], ps_sem.at[2], dev(t_next, j)).start()
            remote(ps_send.at[1], ps_even.at[1, me], ps_sem.at[3], ps_sem.at[2], dev(t_prev, j)).start()
            return carry

        lax.fori_loop(0, n_space, send_near, 0)
        lax.fori_loop(1, n_space, send_group, 0)
        gather(1, 16)
        gather(0, 48)
        write_elementals()
        wait_halo_sends(0, HALF)
        wait_bytes(rs_recv.at[0, :, pl.ds(0, 48)], rs_sem.at[0, 0])
        wait_bytes(rs_recv.at[1, :, pl.ds(0, 16)], rs_sem.at[1, 0])
        wait_bytes(ps_own, ps_sem.at[1])
        total = ps_send[0]
        for k in range(n_space - 1):
            total = total + ps_own[k]
        wait_bytes(ps_own, ps_sem.at[0])
        wait_bytes(ps_even, ps_sem.at[3])
        write_correlators(total)


def solution(mesh):
    n_tm, n_space = mesh.shape["tm"], mesh.shape["space"]
    placed = (
        P("tm", None, None, None, "space"),
        P("tm", None, None, None, None, "space"),
        P("tm", None, None, None, None),
        P(),
        P(),
        P(),
    )

    def body(eigvecs, links, perambulators, directions, mom_pick, mom_table):
        hbm = pl.BlockSpec(memory_space=pl.ANY)
        smem = pl.BlockSpec(memory_space=pltpu.SMEM)
        vmem = pl.BlockSpec(memory_space=pltpu.VMEM)
        dma = pltpu.SemaphoreType.DMA
        return pl.pallas_call(
            functools.partial(kernel, n_tm, n_space),
            out_shape=(
                jax.ShapeDtypeStruct((4, 2, 1, ROWS, NV), F32),
                jax.ShapeDtypeStruct((2, 1, 2, 4, 4), F32),
            ),
            in_specs=[hbm, hbm, hbm, smem, smem, smem],
            out_specs=(vmem, vmem),
            scratch_shapes=[
                pltpu.VMEM((BLOCKS, 2, 3, NV, LANES), BF16),
                pltpu.VMEM((HALF, 2, 3, NV, LANES), BF16),
                pltpu.VMEM((HALF, 2, 3, NV, LANES), BF16),
                pltpu.VMEM((3, 3, 3, 2, BLOCKS * LANES), BF16),
                pltpu.VMEM((3, 3, 2, HALF * LANES), BF16),
                pltpu.VMEM((3, 24, BLOCKS * LANES), F32),
                pltpu.VMEM((24, HALF * LANES), F32),
                pltpu.VMEM((5, 2, 24, LANES), F32),
                pltpu.VMEM((1280, 768), BF16),
                pltpu.VMEM((1280, 768), BF16),
                pltpu.VMEM((512, 768), BF16),
                pltpu.VMEM((1280, 256), F32),
                pltpu.VMEM((512, 256), F32),
                pltpu.VMEM((4, 2, NV, NV), F32),
                pltpu.VMEM((2, n_space, 48, NV), BF16),
                pltpu.VMEM((2, n_space - 1, 48, NV), BF16),
                pltpu.VMEM((2, 48, NV), F32),
                pltpu.VMEM((2, 48, NV), BF16),
                pltpu.VMEM((2, 2, n_space, 48, NV), BF16),
                pltpu.VMEM((2, 2, 512, 512), BF16),
                pltpu.VMEM((2, 2, 512, 512), BF16),
                pltpu.VMEM((4, 768, 512), BF16),
                pltpu.VMEM((2, 4, 2, NV, NV), F32),
                pltpu.VMEM((2, 4, 16, NV), F32),
                pltpu.VMEM((2, 4, 2, NV, NV), BF16),
                pltpu.VMEM((2, 4, 2, NV, NV), BF16),
                pltpu.VMEM((2, 16, NV), F32),
                pltpu.VMEM((n_space - 1, 16, NV), F32),
                pltpu.VMEM((2, n_space, 16, NV), F32),
                dma((3,)),
                dma((2, HALF)),
                dma((2, HALF)),
                dma((2,)),
                dma((2, 2)),
                dma((2, 2)),
                dma((2, 3)),
                dma((2, 2, 2)),
                dma((4,)),
                pltpu.SemaphoreType.REGULAR,
            ],
            compiler_params=pltpu.CompilerParams(
                collective_id=0, has_side_effects=True, vmem_limit_bytes=60 << 20),
            name="elementals_and_correlators",
        )(eigvecs, jnp.transpose(links, (0, 1, 3, 4, 2, 5)), perambulators, directions, mom_pick,
          mom_table.T)

    return jax.shard_map(
        body,
        mesh=mesh,
        in_specs=placed,
        out_specs=(P(None, None, "tm", "space", None), P(None, "tm", None, None, None)),
        check_vma=False,
    )
```

```python
import functools
import math

import jax
import jax.numpy as jnp
from jax import lax
from jax.experimental import pallas as pl
from jax.experimental.pallas import tpu as pltpu
from jax.sharding import PartitionSpec as P

LXY = 48
MESH = pl.DeviceIdType.MESH
F32 = jnp.float32
BF16 = jnp.bfloat16
NT = (((1,), (1,)), ((), ()))
LANES = 128
HALF = 9
BLOCKS = 18
NV = 128
ROWS = 8


def dot_nt(a, b):
    return lax.dot_general(a, b, NT, preferred_element_type=F32)


def kernel(n_tm, n_space, eig, links, tau, dirs, pick, table, elem_out, corr_out,
           vbuf, rdn, rup, lk, lkup, lkf, lkupf, ph, lhs, lhs2, lhsz, acc, accz, part,
           rs_send, rs_recv, own, ag_send, ag, tauo, taun, zbuf, wmat, rowbuf,
           ysend, yrecv, ps_send, ps_own, ps_even, local_sem, halo_send, halo_recv, lk_sem,
           rs_sem, ag_sem, fw_sem, y_sem, ps_sem, go_sem):
    t = lax.axis_index("tm")
    me = lax.axis_index("space")
    odd = lax.rem(t, 2) == 1
    even = lax.rem(t, 2) == 0
    t_next = lax.rem(t + 1, n_tm)
    t_prev = lax.rem(t + n_tm - 1, n_tm)
    up = lax.rem(me + 1, n_space)
    down = lax.rem(me + n_space - 1, n_space)

    def dev(a, b):
        return {"tm": a, "space": b}

    def remote(src, dst, ssem, rsem, where):
        return pltpu.make_async_remote_copy(
            src_ref=src, dst_ref=dst, send_sem=ssem, recv_sem=rsem,
            device_id=where, device_id_type=MESH)

    def wait_bytes(ref, sem):
        pltpu.make_async_copy(ref, ref, sem).wait()

    def load_block(j):
        return pltpu.make_async_copy(
            eig.at[0, :, :, :, pl.ds(pl.multiple_of(j * LANES, LANES), LANES)],
            vbuf.at[j], local_sem.at[0])

    barrier = pltpu.get_barrier_semaphore()

    def greet(a, b):
        pl.semaphore_signal(barrier, inc=1, device_id=dev(a, b), device_id_type=MESH)

    greet(t, up)
    greet(t, down)

    def greet_group(k, carry):
        greet(t, lax.rem(me + k, n_space))
        return carry

    lax.fori_loop(2, n_space - 1, greet_group, 0)

    def greet_near(k, carry):
        greet(t_next, k)
        greet(t_prev, k)
        return carry

    lax.fori_loop(0, n_space, greet_near, 0)
    pltpu.make_async_copy(links.at[0], lk, local_sem.at[1]).start()

    def start_load(j, carry):
        load_block(j).start()
        return carry

    lax.fori_loop(0, BLOCKS, start_load, 0)
    pltpu.make_async_copy(tau.at[0], tauo, local_sem.at[2]).start()

    pl.semaphore_wait(barrier, 3 * n_space - 1)

    def halo(n, side):
        j = n + HALF * side
        return remote(
            eig.at[0, :, :, :, pl.ds(pl.multiple_of(j * LANES, LANES), LANES)],
            (rup if side else rdn).at[n], halo_send.at[side, n], halo_recv.at[side, n],
            dev(t, up if side else down))

    def start_halo(n, carry):
        halo(n, 0).start()
        halo(n, 1).start()
        return carry

    link_copy = remote(links.at[0, 2, :, :, :, pl.ds(HALF * LANES, HALF * LANES)], lkup,
                       lk_sem.at[0], lk_sem.at[1], dev(t, up))
    link_copy.start()

    @pl.when(even)
    def _():
        lax.fori_loop(0, HALF, start_halo, 0)

    site = (lax.broadcasted_iota(jnp.int32, (24, LANES), 0) * LANES
            + lax.broadcasted_iota(jnp.int32, (24, LANES), 1)).astype(F32)
    site_y = jnp.floor((site + 0.5) * (1.0 / LXY))
    site_x = site - site_y * LXY

    def spread_scalar(value):
        return jnp.full((1, LANES), value, jnp.int32)

    picked = []
    for o in range(4):
        choice = spread_scalar(pick[o])
        row = [jnp.zeros((1, LANES), jnp.int32)] * 3
        for r in range(table.shape[1]):
            row = [jnp.where(choice == r, spread_scalar(table[axis, r]), row[axis]) for axis in range(3)]
        picked.append(row)

    def path_momentum(path, axis):
        total = jnp.zeros((1, LANES), jnp.int32)
        for o in range(4):
            total = jnp.where(spread_scalar(dirs[o]) == path, picked[o][axis], total)
        return total.astype(F32)

    mom = [[path_momentum(path, axis) for axis in range(3)] for path in range(4)]
    extent_z = 1.0 * n_space
    plane = me.astype(F32)
    for slot, path, back in ((0, 0, (0, 0, 0)), (1, 1, (1, 0, 0)), (2, 2, (0, 1, 0)),
                             (3, 3, (0, 0, 0)), (4, 3, (0, 0, 1))):
        flat = 2.0 * math.pi * (mom[path][0] * (site_x - back[0]) / LXY
                                + mom[path][1] * (site_y - back[1]) / LXY
                                + mom[path][2] * (plane - back[2]) / extent_z)
        ph[slot, 0] = jnp.cos(flat)
        ph[slot, 1] = jnp.sin(flat)

    wait_bytes(lk, local_sem.at[1])
    flat_x = lax.rem(lax.broadcasted_iota(jnp.int32, (2, BLOCKS * LANES), 1), LXY)
    for d in range(3):
        for c in range(3):
            for a in range(3):
                pair = lk[d, c, a].astype(F32)
                if d == 0:
                    pair = jnp.where(flat_x == 0, pltpu.roll(pair, BLOCKS * LANES - LXY + 1, 1),
                                     pltpu.roll(pair, 1, 1))
                elif d == 1:
                    pair = pltpu.roll(pair, LXY, 1)
                at = (c * 3 + a) * 2
                lkf[d, at:at + 2, :] = pair
    wait_bytes(vbuf, local_sem.at[0])

    acc[...] = jnp.zeros_like(acc)
    accz[...] = jnp.zeros_like(accz)
    lane = lax.broadcasted_iota(jnp.int32, (16, LANES), 1)

    def link_rows(ref, at):
        return [[[jnp.broadcast_to(ref[pl.ds((c * 3 + a) * 2 + ri, 1), at], (8, LANES))
                  for a in range(3)] for c in range(3)] for ri in range(2)]

    def back_block(load, u, slot, j, dst, row, col):
        cosine = jnp.broadcast_to(ph[slot, 0, pl.ds(j, 1), :], (8, LANES))
        sine = jnp.broadcast_to(ph[slot, 1, pl.ds(j, 1), :], (8, LANES))

        def tile(k, carry):
            at = pl.multiple_of(k * 16, 16)
            v = [[load(ri, c, pl.ds(at, 16)) for c in range(3)] for ri in range(2)]
            for a in range(3):
                halves = []
                for h in range(2):
                    w = [[v[ri][c][h * 8:h * 8 + 8] for c in range(3)] for ri in range(2)]
                    b_re = u[0][0][a] * w[0][0] + u[1][0][a] * w[1][0]
                    b_im = u[0][0][a] * w[1][0] - u[1][0][a] * w[0][0]
                    for c in (1, 2):
                        b_re = b_re + u[0][c][a] * w[0][c] + u[1][c][a] * w[1][c]
                        b_im = b_im + u[0][c][a] * w[1][c] - u[1][c][a] * w[0][c]
                    halves.append((cosine * b_re, cosine * b_im, sine * b_re, sine * b_im))
                lanes = pl.ds((col * 3 + a) * LANES, LANES)
                for i in range(4):
                    dst[pl.ds(at + row + i * 128, 16), lanes] = jnp.concatenate(
                        [halves[0][i], halves[1][i]], axis=0).astype(BF16)
            return carry

        lax.fori_loop(0, NV // 16, tile, 0, unroll=True)

    def plain_block(j, dst, col):
        cosine = jnp.broadcast_to(ph[0, 0, pl.ds(j, 1), :], (16, LANES))
        sine = jnp.broadcast_to(ph[0, 1, pl.ds(j, 1), :], (16, LANES))

        def tile(k, carry):
            at = pl.multiple_of(k * 16, 16)
            for c in range(3):
                v_re = vbuf[j, 0, c, pl.ds(at, 16), :].astype(F32)
                v_im = vbuf[j, 1, c, pl.ds(at, 16), :].astype(F32)
                lanes = pl.ds((col * 3 + c) * LANES, LANES)
                dst[pl.ds(at, 16), lanes] = (cosine * v_re + sine * v_im).astype(BF16)
                dst[pl.ds(at + 128, 16), lanes] = (cosine * v_im - sine * v_re).astype(BF16)
            return carry

        lax.fori_loop(0, NV // 16, tile, 0, unroll=True)

    def stacked(parts):
        return jnp.concatenate(
            [jnp.concatenate([p[ri, c] for p in parts for c in range(3)], axis=1) for ri in range(2)],
            axis=0)

    def fill(i, dst):
        for s in range(2):
            j = 2 * i + s
            after = jnp.where(j == BLOCKS - 1, 0, j + 1)
            before = jnp.where(j == 0, BLOCKS - 1, j - 1)
            at = pl.ds(pl.multiple_of(j * LANES, LANES), LANES)
            plain_block(j, dst, s)
            first = lax.rem(j * LANES + lane, LXY) == 0

            def from_x(ri, c, rows):
                here = vbuf[j, ri, c, rows, :].astype(F32)
                near = jnp.where(lane == LANES - 1, vbuf[before, ri, c, rows, :].astype(F32), here)
                far = jnp.where(lane < LXY - 1, vbuf[after, ri, c, rows, :].astype(F32), here)
                return jnp.where(first, pltpu.roll(far, LANES - LXY + 1, 1), pltpu.roll(near, 1, 1))

            def from_y(ri, c, rows):
                return pltpu.roll(jnp.where(lane >= LANES - LXY, vbuf[before, ri, c, rows, :].astype(F32),
                                            vbuf[j, ri, c, rows, :].astype(F32)), LXY, 1)

            back_block(from_x, link_rows(lkf.at[0], at), 1, j, dst, 256, s)
            back_block(from_y, link_rows(lkf.at[1], at), 2, j, dst, 768, s)

    def add_dot(i, src):
        acc[...] += dot_nt(src[...], stacked([vbuf.at[2 * i], vbuf.at[2 * i + 1]]))

    def two_pairs(i, carry):
        fill(2 * i, lhs)
        add_dot(jnp.maximum(2 * i - 1, 0), lhs2)
        fill(2 * i + 1, lhs2)
        add_dot(2 * i, lhs)
        return carry

    lhs2[...] = jnp.zeros_like(lhs2)
    lax.fori_loop(0, BLOCKS // 4, two_pairs, 0)
    fill(BLOCKS // 2 - 1, lhs)
    add_dot(BLOCKS // 2 - 2, lhs2)
    add_dot(BLOCKS // 2 - 1, lhs)

    def blocks_of(ref, row):
        g_rr = ref[row:row + 128, 0:128]
        g_ri = ref[row:row + 128, 128:256]
        g_ir = ref[row + 128:row + 256, 0:128]
        g_ii = ref[row + 128:row + 256, 128:256]
        return g_rr + g_ii, g_ri - g_ir

    def finish_direction(d):
        sums, row = (accz, 0) if d == 2 else (acc, 256 + 512 * d)
        c_re, c_im = blocks_of(sums, row)
        s_re, s_im = blocks_of(sums, row + 256)
        length = (float(LXY), float(LXY), extent_z)[d]
        turn = jnp.full((1, LANES), 2.0 * math.pi / length, F32) * mom[d + 1][d]
        cosine = jnp.cos(turn)
        sine = jnp.sin(turn)
        p_re = c_re - s_im
        p_im = c_im + s_re
        n_re = cosine * p_re - sine * p_im
        n_im = sine * p_re + cosine * p_im
        part[d + 1, 0] = c_re + s_im - n_re.T
        part[d + 1, 1] = c_im - s_re + n_im.T

    plain_re, plain_im = blocks_of(acc, 0)
    part[0, 0] = plain_re.T
    part[0, 1] = -plain_im.T
    finish_direction(0)
    finish_direction(1)

    def spread(first, count, which):
        width = 16 * count
        for j in range(n_space):
            for p in range(count):
                for ri in range(2):
                    own[which, pl.ds(p * 16 + ri * 8, 8), :] = part[first + p, ri, j * 8:(j + 1) * 8, :]
            rs_send[which, j, 0:width, :] = own[which, 0:width, :].astype(BF16)
        for p in range(count):
            for ri in range(2):
                own[which, pl.ds(p * 16 + ri * 8, 8), :] = part[
                    first + p, ri, pl.ds(pl.multiple_of(me * 8, 8), 8), :]

        def send(k, carry):
            j = lax.rem(me + k, n_space)
            remote(rs_send.at[which, j, pl.ds(0, width)], rs_recv.at[which, k - 1, pl.ds(0, width)],
                   rs_sem.at[which, 0], rs_sem.at[which, 1], dev(t, j)).start()
            return carry

        lax.fori_loop(1, n_space, send, 0)

    def gather(which, width):
        wait_bytes(rs_recv.at[which, :, pl.ds(0, width)], rs_sem.at[which, 1])
        total = own[which, 0:width, :]
        for k in range(n_space - 1):
            total = total + rs_recv[which, k, 0:width, :].astype(F32)
        own[which, 0:width, :] = total

    def publish(which, width):
        ag_send[which, 0:width, :] = own[which, 0:width, :].astype(BF16)
        ag[which, 0, me, 0:width, :] = ag_send[which, 0:width, :]

        def send(k, carry):
            remote(ag_send.at[which, pl.ds(0, width)], ag.at[which, 0, me, pl.ds(0, width)],
                   ag_sem.at[which, 0], ag_sem.at[which, 1],
                   dev(t, lax.rem(me + k, n_space))).start()
            return carry

        lax.fori_loop(1, n_space, send, 0)

    def forward(which, width):
        wait_bytes(ag.at[which, 0, pl.ds(0, n_space - 1), pl.ds(0, width)], ag_sem.at[which, 1])
        for side, where in ((0, t_next), (1, t_prev)):
            remote(ag.at[which, 0, :, pl.ds(0, width)], ag.at[which, side, :, pl.ds(0, width)],
                   fw_sem.at[which, side], fw_sem.at[which, 2], dev(where, me)).start()

    def send_weights(which, first_path, count):
        for e, where in ((0, t_prev), (1, t_next)):
            paths = pl.ds(first_path, count)
            remote(ysend.at[e, paths], yrecv.at[e, paths], y_sem.at[which, 0, e], y_sem.at[which, 1, e],
                   dev(where, me)).start()

    def wait_weights(which, first_path, count, side):
        for e in range(2):
            wait_bytes(yrecv.at[e, pl.ds(first_path, count)], y_sem.at[which, side, e])

    @pl.when(even)
    def _():
        spread(0, 3, 0)


    link_copy.wait()
    for c in range(3):
        for a in range(3):
            at = (c * 3 + a) * 2
            lkupf[at:at + 2, :] = lkup[c, a].astype(F32)

    def z_block(n, carry):
        halo(n, 0).wait_recv()
        halo(n, 1).wait_recv()
        at = pl.ds(pl.multiple_of(n * LANES, LANES), LANES)
        m = n + HALF
        back_block(lambda ri, c, rows: vbuf[n, ri, c, rows, :].astype(F32), link_rows(lkf.at[2], at), 3, n, lhsz, 0, 0)
        back_block(lambda ri, c, rows: rup[n, ri, c, rows, :].astype(F32), link_rows(lkupf, at), 4, m, lhsz, 0, 1)
        accz[...] += dot_nt(lhsz[...], stacked([rdn.at[n], vbuf.at[m]]))
        return carry

    def wait_halo_sends(lo, hi):
        def one(n, carry):
            halo(n, 0).wait_send()
            halo(n, 1).wait_send()
            return carry

        lax.fori_loop(lo, hi, one, 0)

    def weights(kind, e, which, count, first_path):
        src = e if kind == 0 else 0
        rows = []
        for p in range(count):
            both = [ag[which, src, j, pl.ds(p * 16, 16), :].astype(F32) for j in range(n_space)]
            phi_re = jnp.concatenate([x[0:8] for x in both], axis=0)
            phi_im = jnp.concatenate([x[8:16] for x in both], axis=0)
            if kind == 0:
                rows += [jnp.concatenate([phi_re, phi_im], axis=1), jnp.concatenate([phi_im, -phi_re], axis=1)]
            else:
                rows += [jnp.concatenate([phi_re, -phi_im], axis=1), jnp.concatenate([phi_im, phi_re], axis=1)]
        phi = jnp.concatenate(rows, axis=0).astype(BF16)
        mat = tauo.at[e] if kind == 0 else taun.at[e]
        for c in range(4):
            col = slice(c * 128, (c + 1) * 128)
            z = dot_nt(jnp.concatenate([mat[0, :, col], mat[1, :, col]], axis=1), phi)
            if kind == 1 and c >= 2:
                z = -z
            z = z.astype(BF16)
            for r in range(4):
                for p in range(2 * count):
                    zbuf[r, p * 128:(p + 1) * 128, col] = z[r * 128:(r + 1) * 128, p * 128:(p + 1) * 128]
        total = None
        for r in range(4):
            row = slice(r * 128, (r + 1) * 128)
            g = dot_nt(zbuf[r, 0:256 * count, :], jnp.concatenate([mat[0, row, :], mat[1, row, :]], axis=0))
            if total is None:
                total = g
            elif kind == 0 and r >= 2:
                total = total - g
            else:
                total = total + g
        for p in range(count):
            one = total[p * 256:(p + 1) * 256]
            rr, ri_, ir, ii = one[0:128, 0:128], one[0:128, 128:256], one[128:256, 0:128], one[128:256, 128:256]
            if kind == 0:
                wmat[e, first_path + p, 0] = rr - ii
                wmat[e, first_path + p, 1] = ri_ + ir
            else:
                ysend[e, first_path + p, 0] = (rr + ii).astype(BF16)
                ysend[e, first_path + p, 1] = (ir - ri_).astype(BF16)

    def weights_of(kind, which, count, first_path):
        for e in range(2):
            weights(kind, e, which, count, first_path)

    def pair_rows(kind, paths, lo, hi):
        mat = wmat if kind == 0 else yrecv
        for e in range(2):
            for p in paths:
                def one(w, carry, e=e, p=p):
                    w_re, w_im = mat[e, w, 0].astype(F32), mat[e, w, 1].astype(F32)
                    p_re, p_im = part[p, 0], part[p, 1]
                    re = jnp.sum(p_re * w_re - p_im * w_im, axis=0, keepdims=True)
                    im = jnp.sum(p_re * w_im + p_im * w_re, axis=0, keepdims=True)
                    if kind == 0:
                        rowbuf[kind, w, pl.ds(e * 4 + p, 1), :] = re
                        rowbuf[kind, w, pl.ds(8 + e * 4 + p, 1), :] = im
                    else:
                        rowbuf[kind, p, pl.ds(e * 4 + w, 1), :] = re
                        rowbuf[kind, p, pl.ds(8 + e * 4 + w, 1), :] = im
                    return carry

                lax.fori_loop(lo, hi, one, 0)

    def write_elementals():
        for o in range(4):
            path = jnp.full((8, LANES), dirs[o], jnp.int32)
            for ri in range(2):
                rows = own[1, ri * 8:(ri + 1) * 8, :]
                for p in range(3):
                    rows = jnp.where(path == p, own[0, p * 16 + ri * 8:p * 16 + ri * 8 + 8, :], rows)
                elem_out[o, ri, 0] = rows

    def write_correlators(total):
        col = lax.broadcasted_iota(jnp.int32, (16, LANES), 1)
        turned = jnp.zeros((16, LANES), F32)
        for q in range(4):
            one = jnp.sum(jnp.where(col == spread_scalar(dirs[q]), total, 0.0), axis=1, keepdims=True)
            turned = jnp.where(col == q, one, turned)
        for o in range(4):
            path = jnp.full((1, LANES), dirs[o], jnp.int32)
            for ri in range(2):
                for e in range(2):
                    at = ri * 8 + e * 4
                    row = turned[at:at + 1]
                    for p in range(1, 4):
                        row = jnp.where(path == p, turned[at + p:at + p + 1], row)
                    corr_out[ri, 0, e, o:o + 1, :] = row[:, 0:4]

    @pl.when(even)
    def _():
        wait_halo_sends(0, 7)
        pl.semaphore_signal(go_sem, inc=1, device_id=dev(t_next, me), device_id_type=MESH)
        lax.fori_loop(0, HALF, z_block, 0)
        finish_direction(2)
        spread(3, 1, 1)
        gather(0, 48)
        publish(0, 48)
        wait_bytes(tauo, local_sem.at[2])
        for e in range(2):
            for ri in range(2):
                taun[e, ri] = tauo[e, ri].T
        gather(1, 16)
        publish(1, 16)
        forward(0, 48)
        weights_of(1, 0, 3, 0)
        send_weights(0, 0, 3)
        forward(1, 16)
        weights_of(1, 1, 1, 3)
        send_weights(1, 3, 1)
        write_elementals()
        wait_halo_sends(7, HALF)
        wait_bytes(rs_recv.at[0, :, pl.ds(0, 48)], rs_sem.at[0, 0])
        wait_bytes(rs_recv.at[1, :, pl.ds(0, 16)], rs_sem.at[1, 0])
        for which, width in ((0, 48), (1, 16)):
            wait_bytes(ag.at[which, 0, pl.ds(0, n_space - 1), pl.ds(0, width)], ag_sem.at[which, 0])
            for side in range(2):
                wait_bytes(ag.at[which, 0, :, pl.ds(0, width)], fw_sem.at[which, side])
        wait_weights(0, 0, 3, 0)
        wait_weights(1, 3, 1, 0)
        wait_bytes(ps_even, ps_sem.at[2])
        row = lax.broadcasted_iota(jnp.int32, (16, LANES), 0)
        first = ps_even[0, 0]
        second = ps_even[1, 0]
        for j in range(1, n_space):
            first = first + ps_even[0, j]
            second = second + ps_even[1, j]
        write_correlators(jnp.where(lax.rem(row, 8) < 4, first, second))

    @pl.when(odd)
    def _():
        pl.semaphore_wait(go_sem, 1)
        lax.fori_loop(0, HALF, start_halo, 0)
        lax.fori_loop(0, 7, z_block, 0)
        wait_bytes(tauo, local_sem.at[2])
        wait_bytes(ag.at[0, :, :, pl.ds(0, 48)], fw_sem.at[0, 2])
        weights_of(0, 0, 3, 0)
        pair_rows(0, (0, 1, 2), 0, 3)
        lax.fori_loop(7, HALF, z_block, 0)
        finish_direction(2)
        spread(3, 1, 1)
        spread(0, 3, 0)
        pair_rows(0, (3,), 0, 3)
        wait_weights(0, 0, 3, 1)
        pair_rows(1, (0, 1, 2, 3), 0, 3)
        wait_bytes(ag.at[1, :, :, pl.ds(0, 16)], fw_sem.at[1, 2])
        weights_of(0, 1, 1, 3)
        pair_rows(0, (0, 1, 2, 3), 3, 4)
        wait_weights(1, 3, 1, 1)
        pair_rows(1, (0, 1, 2, 3), 3, 4)
        col = lax.broadcasted_iota(jnp.int32, (16, LANES), 1)
        for kind in range(2):
            tile = jnp.zeros((16, LANES), F32)
            for q in range(4):
                tile = jnp.where(col == q, jnp.sum(rowbuf[kind, q], axis=1, keepdims=True), tile)
            ps_send[kind] = tile

        def send_group(k, carry):
            remote(ps_send.at[0], ps_own.at[k - 1], ps_sem.at[0], ps_sem.at[1],
                   dev(t, lax.rem(me + k, n_space))).start()
            return carry

        def send_near(j, carry):
            remote(ps_send.at[1], ps_even.at[0, me], ps_sem.at[3], ps_sem.at[2], dev(t_next, j)).start()
            remote(ps_send.at[1], ps_even.at[1, me], ps_sem.at[3], ps_sem.at[2], dev(t_prev, j)).start()
            return carry

        lax.fori_loop(0, n_space, send_near, 0)
        lax.fori_loop(1, n_space, send_group, 0)
        gather(1, 16)
        gather(0, 48)
        write_elementals()
        wait_halo_sends(0, HALF)
        wait_bytes(rs_recv.at[0, :, pl.ds(0, 48)], rs_sem.at[0, 0])
        wait_bytes(rs_recv.at[1, :, pl.ds(0, 16)], rs_sem.at[1, 0])
        wait_bytes(ps_own, ps_sem.at[1])
        total = ps_send[0]
        for k in range(n_space - 1):
            total = total + ps_own[k]
        wait_bytes(ps_own, ps_sem.at[0])
        wait_bytes(ps_even, ps_sem.at[3])
        write_correlators(total)


def solution(mesh):
    n_tm, n_space = mesh.shape["tm"], mesh.shape["space"]
    placed = (
        P("tm", None, None, None, "space"),
        P("tm", None, None, None, None, "space"),
        P("tm", None, None, None, None),
        P(),
        P(),
        P(),
    )

    def body(eigvecs, links, perambulators, directions, mom_pick, mom_table):
        hbm = pl.BlockSpec(memory_space=pl.ANY)
        smem = pl.BlockSpec(memory_space=pltpu.SMEM)
        vmem = pl.BlockSpec(memory_space=pltpu.VMEM)
        dma = pltpu.SemaphoreType.DMA
        return pl.pallas_call(
            functools.partial(kernel, n_tm, n_space),
            out_shape=(
                jax.ShapeDtypeStruct((4, 2, 1, ROWS, NV), F32),
                jax.ShapeDtypeStruct((2, 1, 2, 4, 4), F32),
            ),
            in_specs=[hbm, hbm, hbm, smem, smem, smem],
            out_specs=(vmem, vmem),
            scratch_shapes=[
                pltpu.VMEM((BLOCKS, 2, 3, NV, LANES), BF16),
                pltpu.VMEM((HALF, 2, 3, NV, LANES), BF16),
                pltpu.VMEM((HALF, 2, 3, NV, LANES), BF16),
                pltpu.VMEM((3, 3, 3, 2, BLOCKS * LANES), BF16),
                pltpu.VMEM((3, 3, 2, HALF * LANES), BF16),
                pltpu.VMEM((3, 24, BLOCKS * LANES), F32),
                pltpu.VMEM((24, HALF * LANES), F32),
                pltpu.VMEM((5, 2, 24, LANES), F32),
                pltpu.VMEM((1280, 768), BF16),
                pltpu.VMEM((1280, 768), BF16),
                pltpu.VMEM((512, 768), BF16),
                pltpu.VMEM((1280, 256), F32),
                pltpu.VMEM((512, 256), F32),
                pltpu.VMEM((4, 2, NV, NV), F32),
                pltpu.VMEM((2, n_space, 48, NV), BF16),
                pltpu.VMEM((2, n_space - 1, 48, NV), BF16),
                pltpu.VMEM((2, 48, NV), F32),
                pltpu.VMEM((2, 48, NV), BF16),
                pltpu.VMEM((2, 2, n_space, 48, NV), BF16),
                pltpu.VMEM((2, 2, 512, 512), BF16),
                pltpu.VMEM((2, 2, 512, 512), BF16),
                pltpu.VMEM((4, 768, 512), BF16),
                pltpu.VMEM((2, 4, 2, NV, NV), F32),
                pltpu.VMEM((2, 4, 16, NV), F32),
                pltpu.VMEM((2, 4, 2, NV, NV), BF16),
                pltpu.VMEM((2, 4, 2, NV, NV), BF16),
                pltpu.VMEM((2, 16, NV), F32),
                pltpu.VMEM((n_space - 1, 16, NV), F32),
                pltpu.VMEM((2, n_space, 16, NV), F32),
                dma((3,)),
                dma((2, HALF)),
                dma((2, HALF)),
                dma((2,)),
                dma((2, 2)),
                dma((2, 2)),
                dma((2, 3)),
                dma((2, 2, 2)),
                dma((4,)),
                pltpu.SemaphoreType.REGULAR,
            ],
            compiler_params=pltpu.CompilerParams(
                collective_id=0, has_side_effects=True, vmem_limit_bytes=60 << 20),
            name="elementals_and_correlators",
        )(eigvecs, jnp.transpose(links, (0, 1, 3, 4, 2, 5)), perambulators, directions, mom_pick,
          mom_table.T)

    return jax.shard_map(
        body,
        mesh=mesh,
        in_specs=placed,
        out_specs=(P(None, None, "tm", "space", None), P(None, "tm", None, None, None)),
        check_vma=False,
    )
```
